32 devices in a mesh: cand: 8 (over y, x, core), rel: 4 (over z).
Axes of the slice: x: 2, y: 2, z: 4, core: 2. Of those that a mesh axis runs over, the one named last changes fastest.
Arguments:
- source_rows: bfloat16 [65536, 512], P(('cand', 'rel')), may hold values from -6 to 6
- rel_ids: int32 [65536, 1], P(('cand', 'rel')), may hold values from 0 to 7; in each aligned block of 2048 rows (0 to 2047, 2048 to 4095, ...) at most 512 rows name the same one
- relations: bfloat16 [8, 512, 512], P('rel'), may hold values from -0.25 to 0.25
- entities: float32 [8192, 512], P(('cand', 'rel')), may hold values from -0.3 to 0.3
- pos_slot: int32 [65536], P(('cand', 'rel')), may hold values from 0 to 2047
- negatives: int32 [8, 65536, 16], P(None, ('cand', 'rel')), may hold values from 0 to 255
Outputs:
- updated_entities: float32 [8192, 512], P(('cand', 'rel'))
- source_grad: bfloat16 [65536, 512], P(('cand', 'rel'))
- relation_grad: float32 [512, 8, 512], P('cand', 'rel')
The draws below stay inside these ranges and needn't reach their ends.
Inputs may be any that keep to these rules, and one draw needn't show every extreme that they name: `rel_ids`: in each aligned block of 2048 rows (the rows of one device) no relation is named by more than 512 rows, a bound that some block reaches.
All inputs are finite; a program needn't handle non-finite values.
Results may differ from the reference program's by a relative error of at most 0.019.
Values may be sent and summed in bfloat16 or wider, within the bound.
No kernel may reach another device: no remote copies, remote signals or barrier semaphores. Data moves between devices by JAX's collectives and lax.ppermute only.
A program may use at most 128 MiB of HBM per device.

```python
import math
import jax
import jax.numpy as jnp
import numpy as np
from jax import lax

D = 512
PART = 256
SRC_DEV = 2048
REL_DEV = 2
STOPS = 8
NEG = 16
NREL = 8
MOST = 512
SOURCES = 65536
ENTITIES = 8192
N_CAND = 8
N_REL = 4


def set_ends(drawn, stream_key, least, top_value):
    extent = drawn.shape
    place = [jax.random.randint(jax.random.fold_in(stream_key, axis), (), 0, extent[axis]) for axis in range(len(extent))]
    drawn = drawn.at[tuple(place)].set(least)
    longest = extent.index(max(extent))
    place[longest] = (place[longest] + 1) % extent[longest]
    return drawn.at[tuple(place)].set(top_value)


def with_spikes(entries, stream_key, source, target, blocks, factor):
    owner, partner = [(jnp.arange(entries.shape[axis_at]) // (entries.shape[axis_at] // blocks)).reshape([-1 if axis == axis_at else 1 for axis in range(entries.ndim)]) for axis_at in (source, target)]
    chosen = jax.random.permutation(stream_key, blocks)[partner]
    strong = (owner == chosen) | (owner == (partner + blocks // 2) % blocks)
    return jnp.where(strong, factor * entries, entries)


def levels(key, extent, cuts, low, high):
    level, own = 1.0, jax.random.fold_in(key, 6)
    for position, shards_of in cuts:
        heights = jnp.exp(jax.random.uniform(jax.random.fold_in(own, position), (shards_of,), jnp.float32, low / len(cuts), high / len(cuts)))
        level = level * jnp.repeat(heights, extent[position] // shards_of).reshape([-1 if axis == position else 1 for axis in range(len(extent))])
    return level


def shared_out(own_key, own, number, rows, count, top, most, lean):
    ranking = jax.random.permutation(own_key, count)
    crowded, ordinary = portions_of(count, rows * top, most, lean, True), portions_of(count, rows * top, most, lean, False)
    places = jnp.arange(count)

    def named(tallies, rotation):
        used = int((tallies > 0).sum())
        fixed = max(1, used // 4)
        shifted = fixed + (places - fixed + rotation * (used - fixed)) % max(1, count - fixed)
        return jnp.zeros((count,), jnp.int32).at[ranking[jnp.where(places < fixed, places, shifted)]].set(jnp.asarray(tallies, jnp.int32))

    tallies = jnp.where(number % 4 == 0, named(crowded, number // 4), named(ordinary, number - number // 4 - 1))
    mixed = jax.random.permutation(jax.random.fold_in(own, 3), count)
    donor, receiver = mixed[0:count // 2 * 2:2], mixed[1:count // 2 * 2:2]
    slack = jnp.minimum(tallies[donor] - 1, most - tallies[receiver]) // 2
    slack = jnp.where((donor == ranking[0]) | (receiver == ranking[0]) | (tallies[receiver] == 0), 0, jnp.maximum(slack, 0))
    shifted = jax.random.randint(jax.random.fold_in(own, 4), (count // 2,), 0, 1 << 20) % (slack + 1)
    tallies = tallies.at[donor].add(-shifted).at[receiver].add(shifted)
    items = jnp.searchsorted(jnp.cumsum(tallies), jnp.arange(rows * top), side="right").astype(jnp.int32)
    grid = items.reshape(top, rows).T
    grid = grid[jax.random.permutation(jax.random.fold_in(own, 1), rows)]
    rotation = jax.random.randint(jax.random.fold_in(own, 2), (rows, 1), 0, top)
    return jnp.take_along_axis(grid, (jnp.arange(top)[None, :] + rotation) % top, axis=1)


def portions_of(number_of, total, reach, skew, full):
    weights = [(1 << 20) // math.isqrt(rank ** skew) + 1 for rank in range(1, number_of + 1)]
    largest = reach if full else min(reach, max(-(-total // number_of), total * weights[0] // sum(weights)))
    least = 1 if total - largest >= number_of - 1 else 0
    holding, rest = [largest] + [least] * (number_of - 1), total - largest - least * (number_of - 1)
    while rest > 0:
        movable = [i for i in range(1, number_of) if holding[i] < largest] or [i for i in range(1, number_of) if holding[i] < reach]
        pool, budget = sum([weights[i] for i in movable]), rest
        for i in movable:
            extra = min(reach - holding[i], max(1, budget * weights[i] // pool), rest)
            holding[i] = holding[i] + extra
            rest = rest - extra
    return np.array(holding)


def gaussian(rng, dims, deviation, reach, shards=(), kind=jnp.bfloat16):
    array = jax.random.normal(rng, dims, jnp.float32) * deviation
    if len(shards) > 0:
        array = levels(rng, dims, shards, -0.22, 0.18) * array
    return jnp.clip(array, min=-reach, max=reach).astype(kind)


def gaussian_with(key, shape, scale, most, pieces, heavy, kind=jnp.bfloat16):
    entries = scale * jax.random.normal(key, shape, jnp.float32)
    if pieces:
        entries = entries * levels(key, shape, pieces, -0.22, 0.18)
    return jnp.clip(with_spikes(entries, jax.random.fold_in(key, 3), *heavy), -most, most).astype(kind)


def setup_inputs(seed: int = 0) -> dict:
    seeds = jax.random.split(jax.random.key(seed), 7)
    source_rows = gaussian_with(seeds[0], (SOURCES, D), 1.0, 6.0, ((0, 32),), (0, 1, 32, 2.75))
    rel_ids_keys = jax.random.split(jax.random.fold_in(seeds[1], 1), SOURCES // SRC_DEV)
    rel_ids_turns = jax.random.permutation(jax.random.fold_in(seeds[1], 3), SOURCES // SRC_DEV)
    rel_ids = jax.vmap(lambda own, number: shared_out(jax.random.fold_in(seeds[1], 2), own, number, SRC_DEV, NREL, 1, MOST, 2))(rel_ids_keys, rel_ids_turns).reshape((SOURCES, 1))
    relations = gaussian(seeds[2], (NREL, D, D), D ** -0.5, 0.25, ((0, 4),))
    entities = gaussian(seeds[3], (ENTITIES, D), 0.05, 0.3, ((0, 32),), jnp.float32)
    pos_slot = set_ends(jax.random.randint(seeds[4], (SOURCES,), 0, STOPS * PART), jax.random.fold_in(seeds[4], 1), 0, (STOPS * PART) - 1).astype(jnp.int32)
    negatives = set_ends(jax.random.randint(seeds[5], (STOPS, SOURCES, NEG), 0, PART), jax.random.fold_in(seeds[5], 1), 0, PART - 1).astype(jnp.int32)
    return dict(source_rows=source_rows, rel_ids=rel_ids, relations=relations, entities=entities, pos_slot=pos_slot, negatives=negatives)


learn_rate = 0.005


def reference(source_rows, rel_ids, relations, entities, pos_slot, negatives):
    blocks = N_CAND * N_REL
    width = D
    nrel = REL_DEV * N_REL
    most = 2 * SRC_DEV // nrel
    ids = rel_ids[:, 0].reshape(blocks, SRC_DEV)
    onehot = (ids[:, :, None] == jnp.arange(nrel, dtype=jnp.int32)[None, None, :]).astype(jnp.int32)
    rank = jnp.cumsum(onehot, axis=1) - onehot
    slot = (ids * most + jnp.sum(rank * onehot, axis=2)).astype(jnp.int32)
    owner = jnp.broadcast_to(jnp.arange(blocks, dtype=jnp.int32)[:, None], slot.shape)
    rows = source_rows.reshape(blocks, SRC_DEV, width)
    sent = jnp.zeros((blocks, nrel * most, width), source_rows.dtype).at[owner, slot].set(rows)
    sent = sent.reshape(blocks, nrel, most, width)

    def forward(k):
        part_rows = sent[:, k].reshape(blocks * most, width)
        return jnp.dot(part_rows, relations[k], preferred_element_type=jnp.float32).astype(jnp.bfloat16)

    q_slots = lax.map(forward, jnp.arange(nrel))
    q_slots = jnp.transpose(q_slots.reshape(nrel, blocks, most, width), (1, 0, 2, 3)).reshape(blocks, nrel * most, width)
    queries = q_slots[owner, slot]
    queries = queries.reshape(N_CAND, N_REL, SRC_DEV, width)
    qf = queries.astype(jnp.float32)

    state = entities.reshape(N_CAND, N_REL, PART, width)
    acc = jnp.zeros((N_CAND, N_REL, SRC_DEV, width), jnp.float32)
    columns = jnp.arange(PART, dtype=jnp.int32)
    targets = pos_slot.reshape(N_CAND, N_REL, SRC_DEV)
    for stop in range(STOPS):
        if stop > 0:
            state = jnp.roll(state, 1, axis=0)
        wide = state.astype(jnp.bfloat16)
        wf = wide.astype(jnp.float32)
        logits = jnp.einsum('cnid,cnjd->cnij', qf, wf)
        picks = negatives[stop].reshape(N_CAND, N_REL, SRC_DEV, NEG)
        counts = jnp.zeros(logits.shape, jnp.float32)
        for sample in range(NEG):
            counts = counts + (picks[..., sample][..., None] == columns).astype(jnp.float32)
        hits = (targets[..., None] == stop * PART + columns).astype(jnp.float32)
        weight = (counts * jax.nn.sigmoid(logits) - hits * jax.nn.sigmoid(-logits)).astype(jnp.bfloat16)
        weightf = weight.astype(jnp.float32)
        acc = acc + jnp.einsum('cnij,cnjd->cnid', weightf, wf)
        state = state - learn_rate * jnp.einsum('cnij,cnid->cnjd', weightf, qf)
    updated_entities = state.reshape(blocks * PART, width)

    query_grad = acc.astype(jnp.bfloat16).reshape(blocks, SRC_DEV, width)
    gq = jnp.zeros((blocks, nrel * most, width), jnp.bfloat16).at[owner, slot].set(query_grad)
    gq = gq.reshape(blocks, nrel, most, width)

    def backward(k):
        gq_rows = gq[:, k].reshape(blocks * most, width)
        src = sent[:, k].reshape(blocks * most, width)
        back = jnp.dot(gq_rows, relations[k].T, preferred_element_type=jnp.float32).astype(jnp.bfloat16)
        dmat = jnp.dot(src.T, gq_rows, preferred_element_type=jnp.float32)
        return back, dmat

    back, dmats = lax.map(backward, jnp.arange(nrel))
    back = jnp.transpose(back.reshape(nrel, blocks, most, width), (1, 0, 2, 3)).reshape(blocks, nrel * most, width)
    source_grad = back[owner, slot].reshape(blocks * SRC_DEV, width)
    relation_grad = jnp.transpose(dmats, (1, 0, 2))
    return updated_entities, source_grad, relation_grad
```

```python
import jax
import jax.numpy as jnp
from jax import lax
from jax.experimental import pallas as pl
from jax.experimental.pallas import tpu as pltpu
from jax.sharding import PartitionSpec as P

learn_rate = 0.005
ALIGN = 16
HALVES = 2
bf16 = jnp.bfloat16
f32 = jnp.float32
VMEM_LIMIT = 56 * 2**20


def shift(x, axis, distance):
    n = lax.axis_size(axis)
    return lax.ppermute(x, axis, [((i + distance) % n, i) for i in range(n)])


def swap(x, bit):
    return lax.ppermute(x, "cand", [(i, i ^ bit) for i in range(lax.axis_size("cand"))])


def chip_bits():
    bits, bit = [], 2
    while bit < lax.axis_size("cand"):
        bits.append(bit)
        bit *= 2
    return bits


def bit_orders():
    bits = chip_bits()
    return bits, bits[::-1]


def vmem():
    return pl.BlockSpec(memory_space=pltpu.VMEM)


def smem():
    return pl.BlockSpec(memory_space=pltpu.SMEM)


def call(kernel, out_shape, in_specs, scratch=(), flops=0, moved=0):
    return pl.pallas_call(
        kernel,
        out_shape=out_shape,
        in_specs=in_specs,
        out_specs=jax.tree.map(lambda _: vmem(), out_shape),
        scratch_shapes=scratch,
        compiler_params=pltpu.CompilerParams(vmem_limit_bytes=VMEM_LIMIT),
        cost_estimate=pl.CostEstimate(flops=flops, bytes_accessed=moved, transcendentals=0),
    )


def gather_pieces(relations):
    n, m = lax.axis_size("cand"), lax.axis_size("rel")
    width = relations.shape[-1]
    flat = relations.reshape(-1, width)
    piece = flat.shape[0] // n
    own = lax.dynamic_slice(flat, (lax.axis_index("cand") * piece, 0), (piece, width))
    came = jnp.stack([shift(own, "rel", j) for j in range(1, m)])
    half = piece // 2
    pieces = []
    for h, order in enumerate(bit_orders()):
        held = came[None, :, h * half : (h + 1) * half]
        for bit in order:
            held = jnp.concatenate([held, swap(held, bit)], 0)
        pieces.append(jnp.concatenate([held, swap(held, 1)], 0))
    return pieces


def piece_slots():
    n = lax.axis_size("cand")
    apart = jnp.arange(n, dtype=jnp.int32) ^ lax.axis_index("cand")
    tables = []
    for order in bit_orders():
        slot = jnp.zeros_like(apart)
        for place, bit in enumerate(order + [1]):
            slot = slot + jnp.where((apart & bit) != 0, 1 << place, 0)
        tables.append(slot)
    return jnp.stack(tables).astype(jnp.int32)


def load_matrix(k, me_rel, slots, relations, pieces, matrix, m):
    rel_dev, width = relations.shape[0], relations.shape[1]
    owner, which = k // rel_dev, k % rel_dev
    half = pieces[0].shape[2]
    per = width // (2 * half)
    away = lax.rem(owner - me_rel + m, m)

    @pl.when(away == 0)
    def _():
        matrix[...] = relations[which]

    @pl.when(away != 0)
    def _():
        for i in range(per):
            c = which * per + i
            for h in range(2):
                at = (2 * i + h) * half
                matrix[at : at + half, :] = pieces[h][slots[h, c], away - 1]


def group_rows(k, starts, counts, rows, most):
    first = starts[k]
    low = pl.multiple_of(jnp.minimum(first, rows - most), ALIGN)
    return low, first - low, counts[k]


def project(x, starts, counts, relations, pieces, transposed):
    m = lax.axis_size("rel")
    nrel = relations.shape[0] * m
    rows, width = x.shape
    most = 2 * (rows - nrel * ALIGN) // nrel
    me = lax.axis_index("rel").astype(jnp.int32).reshape(1)

    def kernel(me_ref, slots, starts_ref, counts_ref, x_ref, rel_ref, p0, p1, out_ref, matrix):
        out_ref[...] = jnp.zeros_like(out_ref)
        for k in range(nrel):
            load_matrix(k, me_ref[0], slots, rel_ref, (p0, p1), matrix.at[k % 2], m)
            low, skip, _ = group_rows(k, starts_ref, counts_ref, rows, most)
            dims = (((1,), (1 if transposed else 0,)), ((), ()))
            got = lax.dot_general(
                x_ref[pl.ds(low, most), :], matrix[k % 2], dims, preferred_element_type=f32
            ).astype(bf16)
            mine = lax.broadcasted_iota(jnp.int32, (most, 1), 0) >= skip
            out_ref[pl.ds(low, most), :] = jnp.where(mine, got, out_ref[pl.ds(low, most), :])

    return call(
        kernel,
        jax.ShapeDtypeStruct((rows, width), bf16),
        [smem()] * 4 + [vmem()] * 4,
        [pltpu.VMEM((2, width, width), bf16)],
        2 * nrel * most * width * width,
        0,
    )(me, piece_slots(), starts, counts, x, relations, *pieces)


def relation_terms(xs, gs, starts, counts, rel_dev, column):
    n, m = lax.axis_size("cand"), lax.axis_size("rel")
    nrel = rel_dev * m
    rows, width = xs[0].shape
    most = 2 * (rows - nrel * ALIGN) // nrel
    block, wide = width // n, width // 2
    order = bit_orders()[column]
    apart = jnp.arange(n, dtype=jnp.int32) ^ lax.axis_index("cand")
    slot = jnp.zeros_like(apart)
    for place, bit in enumerate([1] + order):
        slot = slot + jnp.where((apart & bit) != 0, n >> (place + 1), 0)
    slot = slot.astype(jnp.int32)
    away = ((lax.axis_index("rel") - jnp.arange(m)) % m).astype(jnp.int32)

    def kernel(slot_ref, away_ref, st0, ct0, st1, ct1, x0, x1, g0, g1, out_ref):
        for k in range(nrel):
            total = None
            for x_ref, g_ref, st, ct in ((x0, g0, st0, ct0), (x1, g1, st1, ct1)):
                low, skip, count = group_rows(k, st, ct, rows, most)
                row = lax.broadcasted_iota(jnp.int32, (most, 1), 0)
                mine = (row >= skip) & (row < skip + count)
                g = g_ref[pl.ds(low, most), column * wide : (column + 1) * wide]
                g = jnp.where(mine, g, jnp.zeros_like(g))
                term = lax.dot_general(
                    x_ref[pl.ds(low, most), :],
                    g,
                    (((0,), (0,)), ((), ())),
                    preferred_element_type=f32,
                )
                total = term if total is None else total + term
            total = total.astype(bf16)
            to, which = away_ref[k // rel_dev], k % rel_dev
            for b in range(n):
                out_ref[slot_ref[b], to, which] = total[b * block : (b + 1) * block]

    return call(
        kernel,
        jax.ShapeDtypeStruct((n, m, rel_dev, block, wide), bf16),
        [smem()] * 6 + [vmem()] * 4,
        (),
        4 * nrel * most * width * wide,
        0,
    )(slot, away, starts[0], counts[0], starts[1], counts[1], *xs, *gs)


def add(a, b):
    return (a.astype(f32) + b.astype(f32)).astype(bf16)


def reduce_terms(terms, column):
    n, m = lax.axis_size("cand"), lax.axis_size("rel")
    for bit in [1] + bit_orders()[column]:
        half = terms.shape[0] // 2
        terms = add(terms[:half], swap(terms[half:], bit))
    terms = terms[0]
    total = terms[0].astype(f32)
    for j in range(1, m):
        total = total + shift(terms[j], "rel", j).astype(f32)
    return total


def sort_places(rel_ids, nrel):
    ids = rel_ids[:, 0]
    rows = ids.shape[0]
    onehot = ids[None, :] == jnp.arange(nrel, dtype=jnp.int32)[:, None]
    lanes = 128
    blocks = onehot.astype(bf16).reshape(nrel, rows // lanes, lanes)
    upto = (jnp.arange(lanes)[:, None] <= jnp.arange(lanes)[None, :]).astype(bf16)
    within = lax.dot_general(
        blocks, upto, (((2,), (0,)), ((), ())), preferred_element_type=f32
    )
    sums = within[:, :, -1]
    before = jnp.cumsum(sums, axis=1) - sums
    counts = jnp.sum(sums, axis=1).astype(jnp.int32)
    padded = (counts + ALIGN - 1) // ALIGN * ALIGN
    starts = jnp.cumsum(padded) - padded
    rank = (within + before[:, :, None]).reshape(nrel, rows).astype(jnp.int32) - 1
    place = jnp.sum(jnp.where(onehot, rank + starts[:, None], 0), axis=0)
    return place, starts.astype(jnp.int32), counts


def coefficients(picks, stop, where_stop, where_row, part_rows):
    rows = picks.shape[1]
    tile = 128
    sub = 64

    def kernel(picks_ref, stop_ref, row_ref, plus_ref, minus_ref):
        for top in range(0, part_rows, sub):
            column = (lax.broadcasted_iota(jnp.int32, (sub, tile), 0) + (top + 1)).astype(f32).astype(bf16)
            one = jnp.ones((sub, tile), bf16)
            zero = jnp.zeros((sub, tile), bf16)
            for left in range(0, rows, tile):
                count = zero
                for k in range(picks_ref.shape[0]):
                    pick = picks_ref[k : k + 1, left : left + tile]
                    count = count + jnp.where(column == pick, one, zero)
                here = jnp.where(
                    stop_ref[:, left : left + tile] == float(stop + 1), row_ref[:, left : left + tile], 0.0
                ).astype(bf16)
                hit = jnp.where(column == here, one, zero)
                plus_ref[top : top + sub, left : left + tile] = (count + hit) * 0.5
                minus_ref[top : top + sub, left : left + tile] = (count - hit) * 0.5

    shape = jax.ShapeDtypeStruct((part_rows, rows), bf16)
    return call(
        kernel, (shape, shape), [vmem()] * 3, (), 2 * 10**9, 4 * part_rows * rows
    )(picks, where_stop, where_row)


def shards(source_rows, rel_ids, relations, entities, pos_slot, negatives):
    src_rows, width = source_rows.shape
    rel_dev = relations.shape[0]
    n, m = lax.axis_size("cand"), lax.axis_size("rel")
    nrel = rel_dev * m
    stops, _, samples = negatives.shape
    part_rows = entities.shape[0]
    rows = src_rows + nrel * ALIGN
    odd = lax.axis_index("cand") % 2 == 1

    pieces = gather_pieces(relations)

    place, starts, counts = sort_places(rel_ids, nrel)
    onto = (jnp.arange(rows, dtype=jnp.int32)[:, None] == place[None, :]).astype(bf16)
    x_own = jnp.dot(onto, source_rows, preferred_element_type=f32).astype(bf16)
    listed = (jnp.swapaxes(negatives, 1, 2) + 1).reshape(stops * samples, src_rows)
    wanted = jnp.stack([pos_slot // part_rows + 1, pos_slot % part_rows + 1])
    listed = jnp.concatenate([listed, wanted], 0).astype(bf16)
    listed = lax.dot_general(
        listed, onto, (((1,), (1,)), ((), ())), preferred_element_type=f32
    ).astype(bf16)
    picks = listed[: stops * samples].reshape(stops, samples, rows)
    target = listed[stops * samples :]

    x_sib = swap(x_own, 1)
    picks_sib = swap(picks[1::2], 1)
    target_sib = swap(target, 1)
    spans = swap(jnp.stack([starts, counts]), 1)
    starts_sib, counts_sib = spans[0], spans[1]

    plus, minus = [], []
    for stop in range(stops):
        chosen = picks[stop] if stop % 2 == 0 else picks_sib[stop // 2]
        aim = (target if stop % 2 == 0 else target_sib).astype(f32)
        a, b = coefficients(chosen, stop, aim[0:1], aim[1:2], part_rows)
        plus.append(a)
        minus.append(b)

    q_own = project(x_own, starts, counts, relations, pieces, False)
    q_sib = project(x_sib, starts_sib, counts_sib, relations, pieces, False)

    half = part_rows // HALVES
    state = [entities[h * half : (h + 1) * half] for h in range(HALVES)]
    acc = [None, None]
    for stop in range(stops):
        queries = q_own if stop % 2 == 0 else q_sib
        weights, wides = [], []
        for h in range(HALVES):
            cut = slice(h * half, (h + 1) * half)
            wide = state[h].astype(bf16)
            logits = lax.dot_general(
                wide, queries, (((1,), (1,)), ((), ())), preferred_element_type=f32
            )
            weight = (
                plus[stop][cut].astype(f32) * jnp.tanh(0.5 * logits) + minus[stop][cut].astype(f32)
            ).astype(bf16)
            change = jnp.dot(weight, queries, preferred_element_type=f32)
            state[h] = state[h] - learn_rate * change
            weights.append(weight)
            wides.append(wide)
            if stop + 1 < stops:
                moving = 1 - stop % 2
                route = [(i, (i + 2) % n) for i in range(n) if i % 2 == moving]
                came = lax.ppermute(state[h].astype(bf16), "cand", route)
                state[h] = jnp.where(odd == (moving == 1), came.astype(f32), state[h])
        part = lax.dot_general(
            jnp.concatenate(weights, 0),
            jnp.concatenate(wides, 0),
            (((0,), (0,)), ((), ())),
            preferred_element_type=f32,
        )
        acc[stop % 2] = part if acc[stop % 2] is None else acc[stop % 2] + part

    g_own, g_sib = acc[0].astype(bf16), acc[1].astype(bf16)
    grads = []
    for column in range(2):
        terms = relation_terms(
            (x_own, x_sib), (g_own, g_sib), (starts, starts_sib), (counts, counts_sib), rel_dev, column
        )
        grads.append(reduce_terms(terms, column))
    relation_grad = jnp.swapaxes(jnp.concatenate(grads, 2), 0, 1)

    query_grad = (acc[0] + swap(g_sib, 1).astype(f32)).astype(bf16)
    back = project(query_grad, starts, counts, relations, pieces, True)
    source_grad = lax.dot_general(
        onto, back, (((0,), (0,)), ((), ())), preferred_element_type=f32
    ).astype(bf16)
    updated = jnp.concatenate(state, 0)
    if stops % 2 == 0:
        updated = swap(updated, 1)
    return updated, source_grad, relation_grad


def solution(mesh):
    placed = (
        P(("cand", "rel"), None),
        P(("cand", "rel"), None),
        P("rel", None, None),
        P(("cand", "rel"), None),
        P(("cand", "rel")),
        P(None, ("cand", "rel"), None),
    )
    return jax.shard_map(
        shards,
        mesh=mesh,
        in_specs=placed,
        out_specs=(P(("cand", "rel"), None), P(("cand", "rel"), None), P("cand", "rel", None)),
        check_vma=False,
    )
```

```python
import jax
import jax.numpy as jnp
from jax import lax
from jax.experimental import pallas as pl
from jax.experimental.pallas import tpu as pltpu
from jax.sharding import PartitionSpec as P

learn_rate = 0.005
ALIGN = 16
FIELDS = 4
bf16 = jnp.bfloat16
f32 = jnp.float32
VMEM_LIMIT = 14 * 2**20


def shift(x, axis, distance):
    n = lax.axis_size(axis)
    return lax.ppermute(x, axis, [((i + distance) % n, i) for i in range(n)])


def swap(x, bit):
    return lax.ppermute(x, "cand", [(i, i ^ bit) for i in range(lax.axis_size("cand"))])


def chip_bits():
    bits, bit = [], 2
    while bit < lax.axis_size("cand"):
        bits.append(bit)
        bit *= 2
    return bits


def bit_orders():
    bits = chip_bits()
    return bits, bits[::-1]


def vmem():
    return pl.BlockSpec(memory_space=pltpu.VMEM)


def smem():
    return pl.BlockSpec(memory_space=pltpu.SMEM)


def anywhere():
    return pl.BlockSpec(memory_space=pl.ANY)


def call(kernel, out_shape, in_specs, scratch=(), flops=0, moved=0):
    return pl.pallas_call(
        kernel,
        out_shape=out_shape,
        in_specs=in_specs,
        out_specs=jax.tree.map(lambda _: vmem(), out_shape),
        scratch_shapes=scratch,
        compiler_params=pltpu.CompilerParams(vmem_limit_bytes=VMEM_LIMIT),
        cost_estimate=pl.CostEstimate(flops=flops, bytes_accessed=moved, transcendentals=0),
    )


def gather_start(relations):
    n, m = lax.axis_size("cand"), lax.axis_size("rel")
    width = relations.shape[-1]
    flat = relations.reshape(-1, width)
    piece = flat.shape[0] // n
    own = lax.dynamic_slice(flat, (lax.axis_index("cand") * piece, 0), (piece, width))
    came = jnp.stack([shift(own, "rel", j) for j in range(1, m)])
    half = piece // 2
    return [came[None, :, h * half : (h + 1) * half] for h in range(2)]


def gather_step(held, step):
    return [
        jnp.concatenate([part, swap(part, order[step])], 0) for part, order in zip(held, bit_orders())
    ]


def piece_slots():
    n = lax.axis_size("cand")
    apart = jnp.arange(n, dtype=jnp.int32) ^ lax.axis_index("cand")
    tables = []
    for order in bit_orders():
        slot = jnp.zeros_like(apart)
        for place, bit in enumerate(order):
            slot = slot + jnp.where((apart & bit) != 0, 1 << place, 0)
        tables.append(slot)
    return jnp.stack(tables + [apart & 1]).astype(jnp.int32)


def group_rows(k, starts, counts, rows, most):
    first = starts[k]
    low = pl.multiple_of(jnp.minimum(first, rows - most), ALIGN)
    return low, first - low, counts[k]


def project(x, starts, counts, relations, near, far, transposed, fresh):
    m = lax.axis_size("rel")
    rel_dev = relations.shape[0]
    nrel = rel_dev * m
    rows, width = x.shape
    most = 2 * (rows - nrel * ALIGN) // nrel
    half = near.shape[3]
    per = width // (2 * half)
    dims = (((1,), (1 if transposed else 0,)), ((), ()))
    me = lax.axis_index("rel").astype(jnp.int32).reshape(1)

    def kernel(me_ref, slots, starts_ref, counts_ref, *rest):
        given, out_ref, held = rest[:4], rest[4], rest[5:]
        copies = []
        if not fresh:
            copies = [pltpu.make_async_copy(given[i], held[i], held[4].at[i]) for i in range(4)]
        for copy in copies:
            copy.start()
        x_ref, rel_ref, near_ref, far_ref = given if fresh else held[:4]
        out_ref[...] = jnp.zeros_like(out_ref)
        for copy in copies[:2]:
            copy.wait()
        row = lax.broadcasted_iota(jnp.int32, (most, 1), 0)
        for away in range(m):
            if away == 1:
                for copy in copies[2:]:
                    copy.wait()
            for which in range(rel_dev):
                if away == 0:
                    matrix = rel_ref[which]
                else:
                    parts = []
                    for c in range(which * per, which * per + per):
                        for h in range(2):
                            at = slots[h, c]
                            parts.append(
                                jnp.where(slots[2, c] == 1, far_ref[h, at, away - 1], near_ref[h, at, away - 1])
                            )
                    matrix = jnp.concatenate(parts, 0)
                k = lax.rem(me_ref[0] + away, m) * rel_dev + which
                low, skip, count = group_rows(k, starts_ref, counts_ref, rows, most)
                got = lax.dot_general(
                    x_ref[pl.ds(low, most), :], matrix, dims, preferred_element_type=f32
                ).astype(bf16)
                mine = (row >= skip) & (row < skip + count)
                out_ref[pl.ds(low, most), :] = jnp.where(mine, got, out_ref[pl.ds(low, most), :])

    return pl.pallas_call(
        kernel,
        out_shape=jax.ShapeDtypeStruct((rows, width), bf16),
        in_specs=[smem()] * 4 + [vmem() if fresh else anywhere()] * 4,
        out_specs=vmem(),
        scratch_shapes=[]
        if fresh
        else [
            pltpu.VMEM(x.shape, bf16),
            pltpu.VMEM(relations.shape, bf16),
            pltpu.VMEM(near.shape, bf16),
            pltpu.VMEM(far.shape, bf16),
            pltpu.SemaphoreType.DMA((4,)),
        ],
        compiler_params=pltpu.CompilerParams(vmem_limit_bytes=(13 if fresh else 60) * 2**20),
        cost_estimate=pl.CostEstimate(
            flops=2 * nrel * most * width * width, bytes_accessed=8 * 2**20, transcendentals=0
        ),
    )(me, piece_slots(), starts, counts, x, relations, near, far)


def relation_terms(xs, gs, starts, counts, rel_dev, column):
    n, m = lax.axis_size("cand"), lax.axis_size("rel")
    nrel = rel_dev * m
    rows, width = xs[0].shape
    most = 2 * (rows - nrel * ALIGN) // nrel
    block, wide = width // n, width // 2
    order = bit_orders()[column]
    apart = jnp.arange(n, dtype=jnp.int32) ^ lax.axis_index("cand")
    slot = jnp.zeros_like(apart)
    for place, bit in enumerate([1] + order):
        slot = slot + jnp.where((apart & bit) != 0, n >> (place + 1), 0)
    slot = slot.astype(jnp.int32)
    away = ((lax.axis_index("rel") - jnp.arange(m)) % m).astype(jnp.int32)

    def kernel(slot_ref, away_ref, st0, ct0, st1, ct1, x0, x1, g0, g1, out_ref):
        for k in range(nrel):
            total = None
            for x_ref, g_ref, st, ct in ((x0, g0, st0, ct0), (x1, g1, st1, ct1)):
                low, skip, count = group_rows(k, st, ct, rows, most)
                row = lax.broadcasted_iota(jnp.int32, (most, 1), 0)
                mine = (row >= skip) & (row < skip + count)
                g = g_ref[pl.ds(low, most), column * wide : (column + 1) * wide]
                g = jnp.where(mine, g, jnp.zeros_like(g))
                term = lax.dot_general(
                    x_ref[pl.ds(low, most), :],
                    g,
                    (((0,), (0,)), ((), ())),
                    preferred_element_type=f32,
                )
                total = term if total is None else total + term
            total = total.astype(bf16)
            to, which = away_ref[k // rel_dev], k % rel_dev
            for b in range(n):
                out_ref[slot_ref[b], to, which] = total[b * block : (b + 1) * block]

    return call(
        kernel,
        jax.ShapeDtypeStruct((n, m, rel_dev, block, wide), bf16),
        [smem()] * 6 + [vmem()] * 4,
        (),
        4 * nrel * most * width * wide,
        0,
    )(slot, away, starts[0], counts[0], starts[1], counts[1], *xs, *gs)


def add(a, b):
    return (a.astype(f32) + b.astype(f32)).astype(bf16)


def reduce_step(terms, bit):
    half = terms.shape[0] // 2
    return add(terms[:half], swap(terms[half:], bit))


def reduce_rel(terms):
    m = lax.axis_size("rel")
    total = terms[0].astype(f32)
    for j in range(1, m):
        total = total + shift(terms[j], "rel", j).astype(f32)
    return total


def sort_places(rel_ids, nrel):
    ids = rel_ids[:, 0]
    rows = ids.shape[0]
    onehot = ids[None, :] == jnp.arange(nrel, dtype=jnp.int32)[:, None]
    lanes = 128
    blocks = onehot.astype(bf16).reshape(nrel, rows // lanes, lanes)
    upto = (jnp.arange(lanes)[:, None] <= jnp.arange(lanes)[None, :]).astype(bf16)
    within = lax.dot_general(
        blocks, upto, (((2,), (0,)), ((), ())), preferred_element_type=f32
    )
    sums = within[:, :, -1]
    before = jnp.cumsum(sums, axis=1) - sums
    counts = jnp.sum(sums, axis=1).astype(jnp.int32)
    padded = (counts + ALIGN - 1) // ALIGN * ALIGN
    starts = jnp.cumsum(padded) - padded
    rank = (within + before[:, :, None]).reshape(nrel, rows).astype(jnp.int32) - 1
    place = jnp.sum(jnp.where(onehot, rank + starts[:, None], 0), axis=0)
    return place, starts.astype(jnp.int32), counts


def sample_fields(picks, target, stop, part_rows):
    groups, bits = part_rows // FIELDS, picks.shape[0].bit_length()
    picks = picks.astype(jnp.int32) - 1
    target = target.astype(jnp.int32)
    held = jnp.where(picks >= 0, jnp.left_shift(1, bits * (jnp.maximum(picks, 0) // groups)), 0)
    row = jnp.maximum(target[1:2] - 1, 0)
    field = row // groups
    flag = jnp.left_shift(1, bits * field) + jnp.left_shift(1, bits * FIELDS + field)
    group = jnp.concatenate([jnp.maximum(picks, 0), row], 0) % groups
    addend = jnp.concatenate([held, jnp.where(target[0:1] == stop + 1, flag, 0)], 0)
    return group.astype(jnp.int32), addend.astype(jnp.int32)


def coefficients(group, addend, part_rows):
    entries, rows = group.shape
    groups, bits = part_rows // FIELDS, (entries - 1).bit_length()
    lanes = 128

    def kernel(group_ref, addend_ref, plus_ref, minus_ref):
        mine = lax.broadcasted_iota(jnp.int32, (groups, lanes), 0)
        for left in range(0, rows, lanes):
            cols = slice(left, left + lanes)
            packed = jnp.zeros((groups, lanes), jnp.int32)
            for k in range(entries):
                packed = packed + jnp.where(
                    mine == group_ref[k : k + 1, cols], addend_ref[k : k + 1, cols], 0
                )
            for f in range(FIELDS):
                both = ((packed >> (bits * f)) & ((1 << bits) - 1)).astype(f32) * 0.5
                hit = ((packed >> (bits * FIELDS + f)) & 1).astype(f32)
                plus_ref[f * groups : (f + 1) * groups, cols] = both.astype(bf16)
                minus_ref[f * groups : (f + 1) * groups, cols] = (both - hit).astype(bf16)

    shape = jax.ShapeDtypeStruct((part_rows, rows), bf16)
    return call(
        kernel, (shape, shape), [vmem()] * 2, (), 10**9, 4 * part_rows * rows
    )(group, addend)


def shards(source_rows, rel_ids, relations, entities, pos_slot, negatives):
    src_rows, width = source_rows.shape
    rel_dev = relations.shape[0]
    n, m = lax.axis_size("cand"), lax.axis_size("rel")
    nrel = rel_dev * m
    stops, _, samples = negatives.shape
    part_rows = entities.shape[0]
    rows = src_rows + nrel * ALIGN
    odd = lax.axis_index("cand") % 2 == 1

    held = gather_start(relations)

    place, starts, counts = sort_places(rel_ids, nrel)
    onto = (jnp.arange(rows, dtype=jnp.int32)[:, None] == place[None, :]).astype(bf16)
    listed = (jnp.swapaxes(negatives, 1, 2) + 1).reshape(stops * samples, src_rows)
    wanted = jnp.stack([pos_slot // part_rows + 1, pos_slot % part_rows + 1])
    listed = jnp.concatenate([listed, wanted], 0).astype(bf16)
    listed = lax.dot_general(
        listed, onto, (((1,), (1,)), ((), ())), preferred_element_type=f32
    ).astype(bf16)
    listed = jnp.concatenate(
        [listed[:-2].reshape(stops, samples, rows)[i::2].reshape(-1, rows) for i in range(2)] + [listed[-2:]], 0
    )
    even = (stops + 1) // 2 * samples
    listed_own = jnp.concatenate([listed[:even], listed[-2:]], 0)
    listed_sib = swap(listed[even:], 1)

    spans = swap(jnp.stack([starts, counts]), 1)
    starts_sib, counts_sib = spans[0], spans[1]

    picks = (listed_own[:-2].reshape(-1, samples, rows), listed_sib[:-2].reshape(-1, samples, rows))
    targets = (listed_own[-2:], listed_sib[-2:])
    made = {}

    def prepare(stop, after):
        if stop < stops:
            group, addend = sample_fields(picks[stop % 2][stop // 2], targets[stop % 2], stop, part_rows)
            group, addend, _ = lax.optimization_barrier((group, addend, after))
            made[stop] = coefficients(group, addend, part_rows)

    steps = len(chip_bits())
    for step in range(steps):
        held = gather_step(held, step)
        if step == 0:
            held[0], held[1], source_rows = lax.optimization_barrier((held[0], held[1], source_rows))
            x_own = jnp.dot(onto, source_rows, preferred_element_type=f32).astype(bf16)
            x_sib = swap(x_own, 1)
    near = jnp.stack(held)
    first = entities.astype(bf16)
    near, x_own, first = lax.optimization_barrier((near, x_own, first))
    prepare(0, near)
    far = swap(near, 1)
    far, made[0] = lax.optimization_barrier((far, made[0]))
    q_own = project(x_own, starts, counts, relations, near, far, False, True)
    q_sib = project(x_sib, starts_sib, counts_sib, relations, near, far, False, True)

    state = entities
    parts = [[], []]
    acc = [None, None]
    for stop in range(stops):
        mine = stop % 2
        queries = (q_own, q_sib)[mine]
        plus, minus = made[stop]
        wide = state.astype(bf16) if stop else first
        logits = lax.dot_general(
            wide, queries, (((1,), (1,)), ((), ())), preferred_element_type=f32
        )
        weight = (
            plus.astype(f32) * jnp.tanh(0.5 * logits) + minus.astype(f32)
        ).astype(bf16)
        for ahead in (1, 2) if stop == 0 else (1,) if stop > 1 else ():
            prepare(stop + ahead, weight)
        state = state - learn_rate * jnp.dot(weight, queries, preferred_element_type=f32)
        if stop + 1 < stops:
            moving = 1 - mine
            route = [(i, (i + 2) % n) for i in range(n) if i % 2 == moving]
            came = lax.ppermute(state.astype(bf16), "cand", route)
            state = jnp.where(odd == (moving == 1), came.astype(f32), state)
        parts[mine].append((weight, wide))
        if stop == 2:
            nothing = weight[0, 0] * 0
            x_own, x_sib = x_own + nothing, x_sib + nothing
        if stop in (stops - 4, stops - 3, stops - 2, stops - 1):
            part = lax.dot_general(
                jnp.concatenate([w for w, _ in parts[mine]], 0),
                jnp.concatenate([w for _, w in parts[mine]], 0),
                (((0,), (0,)), ((), ())),
                preferred_element_type=f32,
            )
            acc[mine] = part if acc[mine] is None else acc[mine] + part
            parts[mine] = []

    g_own, g_sib = acc[0].astype(bf16), acc[1].astype(bf16)
    terms = []
    for column in range(2):
        raw = relation_terms(
            (x_own, x_sib), (g_own, g_sib), (starts, starts_sib), (counts, counts_sib), rel_dev, column
        )
        terms.append(reduce_step(raw, 1))
    begun = terms[1]
    for step in range(steps):
        terms = [reduce_step(part, order[step]) for part, order in zip(terms, bit_orders())]
    relation_grad = reduce_rel(jnp.concatenate([part[0] for part in terms], -1))
    relation_grad = jnp.swapaxes(relation_grad, 0, 1)

    query_grad = (acc[0] + swap(g_sib, 1).astype(f32)).astype(bf16)
    query_grad, _ = lax.optimization_barrier((query_grad, begun))
    back = project(query_grad, starts, counts, relations, near, far, True, False)
    source_grad = lax.dot_general(
        onto, back, (((0,), (0,)), ((), ())), preferred_element_type=f32
    ).astype(bf16)
    updated = swap(state, 1) if stops % 2 == 0 else state
    return updated, source_grad, relation_grad


def solution(mesh):
    placed = (
        P(("cand", "rel"), None),
        P(("cand", "rel"), None),
        P("rel", None, None),
        P(("cand", "rel"), None),
        P(("cand", "rel")),
        P(None, ("cand", "rel"), None),
    )
    return jax.shard_map(
        shards,
        mesh=mesh,
        in_specs=placed,
        out_specs=(P(("cand", "rel"), None), P(("cand", "rel"), None), P("cand", "rel", None)),
        check_vma=False,
    )
```

```python
import jax
import jax.numpy as jnp
from jax import lax
from jax.experimental import pallas as pl
from jax.experimental.pallas import tpu as pltpu
from jax.sharding import PartitionSpec as P

learn_rate = 0.005
ALIGN = 16
FIELDS = 4
bf16 = jnp.bfloat16
f32 = jnp.float32
VMEM_LIMIT = 14 * 2**20


def shift(x, axis, distance):
    n = lax.axis_size(axis)
    return lax.ppermute(x, axis, [((i + distance) % n, i) for i in range(n)])


def swap(x, bit):
    return lax.ppermute(x, "cand", [(i, i ^ bit) for i in range(lax.axis_size("cand"))])


def chip_bits():
    bits, bit = [], 2
    while bit < lax.axis_size("cand"):
        bits.append(bit)
        bit *= 2
    return bits


def bit_orders():
    bits = chip_bits()
    return bits, bits[::-1]


def vmem():
    return pl.BlockSpec(memory_space=pltpu.VMEM)


def smem():
    return pl.BlockSpec(memory_space=pltpu.SMEM)


def anywhere():
    return pl.BlockSpec(memory_space=pl.ANY)


def call(kernel, out_shape, in_specs, scratch=(), flops=0, moved=0):
    return pl.pallas_call(
        kernel,
        out_shape=out_shape,
        in_specs=in_specs,
        out_specs=jax.tree.map(lambda _: vmem(), out_shape),
        scratch_shapes=scratch,
        compiler_params=pltpu.CompilerParams(vmem_limit_bytes=VMEM_LIMIT),
        cost_estimate=pl.CostEstimate(flops=flops, bytes_accessed=moved, transcendentals=0),
    )


def gather_start(relations):
    n, m = lax.axis_size("cand"), lax.axis_size("rel")
    width = relations.shape[-1]
    flat = relations.reshape(-1, width)
    piece = flat.shape[0] // n
    own = lax.dynamic_slice(flat, (lax.axis_index("cand") * piece, 0), (piece, width))
    came = jnp.stack([shift(own, "rel", j) for j in range(1, m)])
    half = piece // 2
    return [came[None, :, h * half : (h + 1) * half] for h in range(2)]


def gather_step(held, step):
    return [
        jnp.concatenate([part, swap(part, order[step])], 0) for part, order in zip(held, bit_orders())
    ]


def piece_slots():
    n = lax.axis_size("cand")
    apart = jnp.arange(n, dtype=jnp.int32) ^ lax.axis_index("cand")
    tables = []
    for order in bit_orders():
        slot = jnp.zeros_like(apart)
        for place, bit in enumerate(order):
            slot = slot + jnp.where((apart & bit) != 0, 1 << place, 0)
        tables.append(slot)
    return jnp.stack(tables + [apart & 1]).astype(jnp.int32)


def group_rows(k, starts, counts, rows, most):
    first = starts[k]
    low = pl.multiple_of(jnp.minimum(first, rows - most), ALIGN)
    return low, first - low, counts[k]


def project(x, starts, counts, relations, near, far, transposed, fresh):
    m = lax.axis_size("rel")
    rel_dev = relations.shape[0]
    nrel = rel_dev * m
    rows, width = x.shape
    most = 2 * (rows - nrel * ALIGN) // nrel
    half = near.shape[3]
    per = width // (2 * half)
    dims = (((1,), (1 if transposed else 0,)), ((), ()))
    me = lax.axis_index("rel").astype(jnp.int32).reshape(1)

    def kernel(me_ref, slots, starts_ref, counts_ref, *rest):
        given, out_ref, held = rest[:4], rest[4], rest[5:]
        copies = []
        if not fresh:
            copies = [pltpu.make_async_copy(given[i], held[i], held[4].at[i]) for i in range(4)]
        for copy in copies:
            copy.start()
        x_ref, rel_ref, near_ref, far_ref = given if fresh else held[:4]
        out_ref[...] = jnp.zeros_like(out_ref)
        for copy in copies[:2]:
            copy.wait()
        row = lax.broadcasted_iota(jnp.int32, (most, 1), 0)
        for away in range(m):
            if away == 1:
                for copy in copies[2:]:
                    copy.wait()
            for which in range(rel_dev):
                if away == 0:
                    matrix = rel_ref[which]
                else:
                    parts = []
                    for c in range(which * per, which * per + per):
                        for h in range(2):
                            at = slots[h, c]
                            parts.append(
                                jnp.where(slots[2, c] == 1, far_ref[h, at, away - 1], near_ref[h, at, away - 1])
                            )
                    matrix = jnp.concatenate(parts, 0)
                k = lax.rem(me_ref[0] + away, m) * rel_dev + which
                low, skip, count = group_rows(k, starts_ref, counts_ref, rows, most)
                got = lax.dot_general(
                    x_ref[pl.ds(low, most), :], matrix, dims, preferred_element_type=f32
                ).astype(bf16)
                mine = (row >= skip) & (row < skip + count)
                out_ref[pl.ds(low, most), :] = jnp.where(mine, got, out_ref[pl.ds(low, most), :])

    return pl.pallas_call(
        kernel,
        out_shape=jax.ShapeDtypeStruct((rows, width), bf16),
        in_specs=[smem()] * 4 + [vmem() if fresh else anywhere()] * 4,
        out_specs=vmem(),
        scratch_shapes=[]
        if fresh
        else [
            pltpu.VMEM(x.shape, bf16),
            pltpu.VMEM(relations.shape, bf16),
            pltpu.VMEM(near.shape, bf16),
            pltpu.VMEM(far.shape, bf16),
            pltpu.SemaphoreType.DMA((4,)),
        ],
        compiler_params=pltpu.CompilerParams(vmem_limit_bytes=(13 if fresh else 60) * 2**20),
        cost_estimate=pl.CostEstimate(
            flops=2 * nrel * most * width * width, bytes_accessed=8 * 2**20, transcendentals=0
        ),
    )(me, piece_slots(), starts, counts, x, relations, near, far)


def relation_terms(xs, gs, starts, counts, rel_dev, column):
    n, m = lax.axis_size("cand"), lax.axis_size("rel")
    nrel = rel_dev * m
    rows, width = xs[0].shape
    most = 2 * (rows - nrel * ALIGN) // nrel
    block, wide = width // n, width // 2
    order = bit_orders()[column]
    apart = jnp.arange(n, dtype=jnp.int32) ^ lax.axis_index("cand")
    slot = jnp.zeros_like(apart)
    for place, bit in enumerate([1] + order):
        slot = slot + jnp.where((apart & bit) != 0, n >> (place + 1), 0)
    slot = slot.astype(jnp.int32)
    away = ((lax.axis_index("rel") - jnp.arange(m)) % m).astype(jnp.int32)

    def kernel(slot_ref, away_ref, st0, ct0, st1, ct1, x0, x1, g0, g1, out_ref):
        for k in range(nrel):
            total = None
            for x_ref, g_ref, st, ct in ((x0, g0, st0, ct0), (x1, g1, st1, ct1)):
                low, skip, count = group_rows(k, st, ct, rows, most)
                row = lax.broadcasted_iota(jnp.int32, (most, 1), 0)
                mine = (row >= skip) & (row < skip + count)
                g = g_ref[pl.ds(low, most), column * wide : (column + 1) * wide]
                g = jnp.where(mine, g, jnp.zeros_like(g))
                term = lax.dot_general(
                    x_ref[pl.ds(low, most), :],
                    g,
                    (((0,), (0,)), ((), ())),
                    preferred_element_type=f32,
                )
                total = term if total is None else total + term
            total = total.astype(bf16)
            to, which = away_ref[k // rel_dev], k % rel_dev
            for b in range(n):
                out_ref[slot_ref[b], to, which] = total[b * block : (b + 1) * block]

    return call(
        kernel,
        jax.ShapeDtypeStruct((n, m, rel_dev, block, wide), bf16),
        [smem()] * 6 + [vmem()] * 4,
        (),
        4 * nrel * most * width * wide,
        0,
    )(slot, away, starts[0], counts[0], starts[1], counts[1], *xs, *gs)


def add(a, b):
    return (a.astype(f32) + b.astype(f32)).astype(bf16)


def reduce_step(terms, bit):
    half = terms.shape[0] // 2
    return add(terms[:half], swap(terms[half:], bit))


def reduce_rel(terms):
    m = lax.axis_size("rel")
    total = terms[0].astype(f32)
    for j in range(1, m):
        total = total + shift(terms[j], "rel", j).astype(f32)
    return total


def sort_places(rel_ids, nrel):
    ids = rel_ids[:, 0]
    rows = ids.shape[0]
    onehot = ids[None, :] == jnp.arange(nrel, dtype=jnp.int32)[:, None]
    lanes = 128
    blocks = onehot.astype(bf16).reshape(nrel, rows // lanes, lanes)
    upto = (jnp.arange(lanes)[:, None] <= jnp.arange(lanes)[None, :]).astype(bf16)
    within = lax.dot_general(
        blocks, upto, (((2,), (0,)), ((), ())), preferred_element_type=f32
    )
    sums = within[:, :, -1]
    before = jnp.cumsum(sums, axis=1) - sums
    counts = jnp.sum(sums, axis=1).astype(jnp.int32)
    padded = (counts + ALIGN - 1) // ALIGN * ALIGN
    starts = jnp.cumsum(padded) - padded
    rank = (within + before[:, :, None]).reshape(nrel, rows).astype(jnp.int32) - 1
    place = jnp.sum(jnp.where(onehot, rank + starts[:, None], 0), axis=0)
    return place, starts.astype(jnp.int32), counts


def sample_fields(picks, target, stop, part_rows):
    groups, bits = part_rows // FIELDS, picks.shape[0].bit_length()
    picks = picks.astype(jnp.int32) - 1
    target = target.astype(jnp.int32)
    held = jnp.where(picks >= 0, jnp.left_shift(1, bits * (jnp.maximum(picks, 0) // groups)), 0)
    row = jnp.maximum(target[1:2] - 1, 0)
    field = row // groups
    flag = jnp.left_shift(1, bits * field) + jnp.left_shift(1, bits * FIELDS + field)
    group = jnp.concatenate([jnp.maximum(picks, 0), row], 0) % groups
    addend = jnp.concatenate([held, jnp.where(target[0:1] == stop + 1, flag, 0)], 0)
    return group.astype(jnp.int32), addend.astype(jnp.int32)


def coefficients(group, addend, part_rows):
    entries, rows = group.shape
    groups, bits = part_rows // FIELDS, (entries - 1).bit_length()
    lanes = 128

    def kernel(group_ref, addend_ref, plus_ref, minus_ref):
        mine = lax.broadcasted_iota(jnp.int32, (groups, lanes), 0)
        for left in range(0, rows, lanes):
            cols = slice(left, left + lanes)
            packed = jnp.zeros((groups, lanes), jnp.int32)
            for k in range(entries):
                packed = packed + jnp.where(
                    mine == group_ref[k : k + 1, cols], addend_ref[k : k + 1, cols], 0
                )
            for f in range(FIELDS):
                both = ((packed >> (bits * f)) & ((1 << bits) - 1)).astype(f32) * 0.5
                hit = ((packed >> (bits * FIELDS + f)) & 1).astype(f32)
                plus_ref[f * groups : (f + 1) * groups, cols] = both.astype(bf16)
                minus_ref[f * groups : (f + 1) * groups, cols] = (both - hit).astype(bf16)

    shape = jax.ShapeDtypeStruct((part_rows, rows), bf16)
    return call(
        kernel, (shape, shape), [vmem()] * 2, (), 10**9, 4 * part_rows * rows
    )(group, addend)


def shards(source_rows, rel_ids, relations, entities, pos_slot, negatives):
    src_rows, width = source_rows.shape
    rel_dev = relations.shape[0]
    n, m = lax.axis_size("cand"), lax.axis_size("rel")
    nrel = rel_dev * m
    stops, _, samples = negatives.shape
    part_rows = entities.shape[0]
    rows = src_rows + nrel * ALIGN
    odd = lax.axis_index("cand") % 2 == 1

    held = gather_start(relations)

    place, starts, counts = sort_places(rel_ids, nrel)
    onto = (jnp.arange(rows, dtype=jnp.int32)[:, None] == place[None, :]).astype(bf16)
    listed = (jnp.swapaxes(negatives, 1, 2) + 1).reshape(stops * samples, src_rows)
    wanted = jnp.stack([pos_slot // part_rows + 1, pos_slot % part_rows + 1])
    listed = jnp.concatenate([listed, wanted], 0).astype(bf16)
    listed = lax.dot_general(
        listed, onto, (((1,), (1,)), ((), ())), preferred_element_type=f32
    ).astype(bf16)
    listed = jnp.concatenate(
        [listed[:-2].reshape(stops, samples, rows)[i::2].reshape(-1, rows) for i in range(2)] + [listed[-2:]], 0
    )
    even = (stops + 1) // 2 * samples
    listed_own = jnp.concatenate([listed[:even], listed[-2:]], 0)
    listed_sib = swap(listed[even:], 1)

    spans = swap(jnp.stack([starts, counts]), 1)
    starts_sib, counts_sib = spans[0], spans[1]

    held[0], listed_own, listed_sib = lax.optimization_barrier((held[0], listed_own, listed_sib))
    picks = (listed_own[:-2].reshape(-1, samples, rows), listed_sib[:-2].reshape(-1, samples, rows))
    targets = (listed_own[-2:], listed_sib[-2:])
    made = {}

    def prepare(stop, after):
        if stop < stops:
            group, addend = sample_fields(picks[stop % 2][stop // 2], targets[stop % 2], stop, part_rows)
            group, addend, _ = lax.optimization_barrier((group, addend, after))
            made[stop] = coefficients(group, addend, part_rows)

    steps = len(chip_bits())
    for step in range(steps):
        held = gather_step(held, step)
        if step == 0:
            held[0], held[1], source_rows = lax.optimization_barrier((held[0], held[1], source_rows))
            x_own = jnp.dot(onto, source_rows, preferred_element_type=f32).astype(bf16)
            x_sib = swap(x_own, 1)
            prepare(0, held[0])
    near = jnp.stack(held)
    first = entities.astype(bf16)
    near, x_own, first, made[0] = lax.optimization_barrier((near, x_own, first, made[0]))
    prepare(1, near)
    far = swap(near, 1)
    far, made[1] = lax.optimization_barrier((far, made[1]))
    q_own = project(x_own, starts, counts, relations, near, far, False, True)
    q_sib = project(x_sib, starts_sib, counts_sib, relations, near, far, False, True)

    state = entities
    parts = [[], []]
    acc = [None, None]
    for stop in range(stops):
        mine = stop % 2
        queries = (q_own, q_sib)[mine]
        plus, minus = made[stop]
        wide = state.astype(bf16) if stop else first
        logits = lax.dot_general(
            wide, queries, (((1,), (1,)), ((), ())), preferred_element_type=f32
        )
        weight = (
            plus.astype(f32) * jnp.tanh(0.5 * logits) + minus.astype(f32)
        ).astype(bf16)
        if stop > 0:
            prepare(stop + 1, weight)
        state = state - learn_rate * jnp.dot(weight, queries, preferred_element_type=f32)
        if stop + 1 < stops:
            moving = 1 - mine
            route = [(i, (i + 2) % n) for i in range(n) if i % 2 == moving]
            came = lax.ppermute(state.astype(bf16), "cand", route)
        parts[mine].append((weight, wide))
        if stop == 2:
            nothing = weight[0, 0] * 0
            x_own, x_sib = x_own + nothing, x_sib + nothing
        if stop >= stops - 4:
            together = list(zip(*parts[mine]))
            part = lax.dot_general(
                jnp.concatenate(together[0], 0),
                jnp.concatenate(together[1], 0),
                (((0,), (0,)), ((), ())),
                preferred_element_type=f32,
            )
            acc[mine] = part if acc[mine] is None else (acc[mine] + part).astype(bf16)
            parts[mine] = []
            if stop + 1 < stops:
                came, acc[mine] = lax.optimization_barrier((came, acc[mine]))
        if stop == 0:
            came, q_sib = lax.optimization_barrier((came, q_sib))
        if stop + 1 < stops:
            state = jnp.where(odd == (moving == 1), came.astype(f32), state)

    g_own, g_sib = acc
    terms = []
    for column in range(2):
        raw = relation_terms(
            (x_own, x_sib), (g_own, g_sib), (starts, starts_sib), (counts, counts_sib), rel_dev, column
        )
        terms.append(reduce_step(raw, 1))
    begun = terms[1]
    query_grad = add(g_own, swap(g_sib, 1))
    query_grad, state, _ = lax.optimization_barrier((query_grad, state, begun))
    back = project(query_grad, starts, counts, relations, near, far, True, False)
    for step in range(steps):
        halves = [part.shape[0] // 2 for part in terms]
        came = [swap(part[half:], order[step]) for part, half, order in zip(terms, halves, bit_orders())]
        if step == 0:
            *came, back = lax.optimization_barrier((*came, back))
            source_grad = lax.dot_general(
                onto, back, (((0,), (0,)), ((), ())), preferred_element_type=f32
            ).astype(bf16)
        if step == 1:
            *came, source_grad = lax.optimization_barrier((*came, source_grad))
        terms = [add(part[:half], other) for part, half, other in zip(terms, halves, came)]
    relation_grad = reduce_rel(jnp.concatenate([part[0] for part in terms], -1))
    relation_grad = jnp.swapaxes(relation_grad, 0, 1)
    updated = swap(state, 1) if stops % 2 == 0 else state
    return updated, source_grad, relation_grad


def solution(mesh):
    placed = (
        P(("cand", "rel"), None),
        P(("cand", "rel"), None),
        P("rel", None, None),
        P(("cand", "rel"), None),
        P(("cand", "rel")),
        P(None, ("cand", "rel"), None),
    )
    return jax.shard_map(
        shards,
        mesh=mesh,
        in_specs=placed,
        out_specs=(P(("cand", "rel"), None), P(("cand", "rel"), None), P("cand", "rel", None)),
        check_vma=False,
    )
```

```python
import jax
import jax.numpy as jnp
from jax import lax
from jax.experimental import pallas as pl
from jax.experimental.pallas import tpu as pltpu
from jax.sharding import PartitionSpec as P

learn_rate = 0.005
ALIGN = 16
FIELDS = 4
bf16 = jnp.bfloat16
f32 = jnp.float32
VMEM_LIMIT = 14 * 2**20


def shift(x, axis, distance):
    n = lax.axis_size(axis)
    return lax.ppermute(x, axis, [((i + distance) % n, i) for i in range(n)])


def swap(x, bit):
    return lax.ppermute(x, "cand", [(i, i ^ bit) for i in range(lax.axis_size("cand"))])


def swap_rel(x, bit):
    return lax.ppermute(x, "rel", [(i, i ^ bit) for i in range(lax.axis_size("rel"))])


def rel_bits():
    return [1 << i for i in range((lax.axis_size("rel") - 1).bit_length())]


def chip_bits():
    bits, bit = [], 2
    while bit < lax.axis_size("cand"):
        bits.append(bit)
        bit *= 2
    return bits


def bit_orders():
    bits = chip_bits()
    return bits, bits[::-1]


def vmem():
    return pl.BlockSpec(memory_space=pltpu.VMEM)


def smem():
    return pl.BlockSpec(memory_space=pltpu.SMEM)


def anywhere():
    return pl.BlockSpec(memory_space=pl.ANY)


def call(kernel, out_shape, in_specs, scratch=(), flops=0, moved=0):
    return pl.pallas_call(
        kernel,
        out_shape=out_shape,
        in_specs=in_specs,
        out_specs=jax.tree.map(lambda _: vmem(), out_shape),
        scratch_shapes=scratch,
        compiler_params=pltpu.CompilerParams(vmem_limit_bytes=VMEM_LIMIT),
        cost_estimate=pl.CostEstimate(flops=flops, bytes_accessed=moved, transcendentals=0),
    )


def gather_start(relations):
    n, m = lax.axis_size("cand"), lax.axis_size("rel")
    width = relations.shape[-1]
    flat = relations.reshape(-1, width)
    piece = flat.shape[0] // n
    own = lax.dynamic_slice(flat, (lax.axis_index("cand") * piece, 0), (piece, width))
    came = jnp.stack([shift(own, "rel", j) for j in range(1, m)])
    half = piece // 2
    return [came[None, :, h * half : (h + 1) * half] for h in range(2)]


def gather_step(held, step):
    return [
        jnp.concatenate([part, swap(part, order[step])], 0) for part, order in zip(held, bit_orders())
    ]


def piece_slots():
    n = lax.axis_size("cand")
    apart = jnp.arange(n, dtype=jnp.int32) ^ lax.axis_index("cand")
    tables = []
    for order in bit_orders():
        slot = jnp.zeros_like(apart)
        for place, bit in enumerate(order):
            slot = slot + jnp.where((apart & bit) != 0, 1 << place, 0)
        tables.append(slot)
    return jnp.stack(tables + [apart & 1]).astype(jnp.int32)


def group_rows(k, starts, counts, rows, most):
    first = starts[k]
    low = pl.multiple_of(jnp.minimum(first, rows - most), ALIGN)
    return low, first - low, counts[k]


def project(x, starts, counts, relations, near, far, transposed, fresh):
    m = lax.axis_size("rel")
    rel_dev = relations.shape[0]
    nrel = rel_dev * m
    rows, width = x.shape
    most = 2 * (rows - nrel * ALIGN) // nrel
    half = near.shape[3]
    per = width // (2 * half)
    dims = (((1,), (1 if transposed else 0,)), ((), ()))
    me = lax.axis_index("rel").astype(jnp.int32).reshape(1)

    def kernel(me_ref, slots, starts_ref, counts_ref, *rest):
        given, out_ref, held = rest[:4], rest[4], rest[5:]
        copies = []
        if not fresh:
            copies = [pltpu.make_async_copy(given[i], held[i], held[4].at[i]) for i in range(4)]
        for copy in copies:
            copy.start()
        x_ref, rel_ref, near_ref, far_ref = given if fresh else held[:4]
        out_ref[...] = jnp.zeros_like(out_ref)
        for copy in copies[:2]:
            copy.wait()
        row = lax.broadcasted_iota(jnp.int32, (most, 1), 0)
        for away in range(m):
            if away == 1:
                for copy in copies[2:]:
                    copy.wait()
            for which in range(rel_dev):
                if away == 0:
                    matrix = rel_ref[which]
                else:
                    parts = []
                    for c in range(which * per, which * per + per):
                        for h in range(2):
                            at = slots[h, c]
                            parts.append(
                                jnp.where(slots[2, c] == 1, far_ref[h, at, away - 1], near_ref[h, at, away - 1])
                            )
                    matrix = jnp.concatenate(parts, 0)
                k = lax.rem(me_ref[0] + away, m) * rel_dev + which
                low, skip, count = group_rows(k, starts_ref, counts_ref, rows, most)
                got = lax.dot_general(
                    x_ref[pl.ds(low, most), :], matrix, dims, preferred_element_type=f32
                ).astype(bf16)
                mine = (row >= skip) & (row < skip + count)
                out_ref[pl.ds(low, most), :] = jnp.where(mine, got, out_ref[pl.ds(low, most), :])

    return pl.pallas_call(
        kernel,
        out_shape=jax.ShapeDtypeStruct((rows, width), bf16),
        in_specs=[smem()] * 4 + [vmem() if fresh else anywhere()] * 4,
        out_specs=vmem(),
        scratch_shapes=[]
        if fresh
        else [
            pltpu.VMEM(x.shape, bf16),
            pltpu.VMEM(relations.shape, bf16),
            pltpu.VMEM(near.shape, bf16),
            pltpu.VMEM(far.shape, bf16),
            pltpu.SemaphoreType.DMA((4,)),
        ],
        compiler_params=pltpu.CompilerParams(vmem_limit_bytes=(13 if fresh else 60) * 2**20),
        cost_estimate=pl.CostEstimate(
            flops=2 * nrel * most * width * width, bytes_accessed=8 * 2**20, transcendentals=0
        ),
    )(me, piece_slots(), starts, counts, x, relations, near, far)


def far_first(apart, bits):
    place = jnp.zeros_like(apart)
    for i, bit in enumerate(bits):
        place = place + jnp.where((apart & bit) != 0, 1 << (len(bits) - 1 - i), 0)
    return place.astype(jnp.int32)


def relation_terms(xs, gs, starts, counts, rel_dev, which):
    n, m = lax.axis_size("cand"), lax.axis_size("rel")
    nrel = rel_dev * m
    rows, width = xs[0].shape
    most = 2 * (rows - nrel * ALIGN) // nrel
    block, wide = width // n, width // 2
    me = lax.axis_index("cand")
    apart = (jnp.arange(n // 2, dtype=jnp.int32) ^ (me // 2)) * 2
    slot = jnp.stack([far_first(apart, order) for order in bit_orders()])
    away = far_first(jnp.arange(m, dtype=jnp.int32) ^ lax.axis_index("rel"), rel_bits())
    core = (me % 2).astype(jnp.int32).reshape(1)

    def kernel(core_ref, slot_ref, away_ref, st0, ct0, st1, ct1, x0, x1, g0, g1, keep_ref, send_ref):
        row = lax.broadcasted_iota(jnp.int32, (most, 1), 0)
        second = core_ref[0] == 1
        for owner in range(m):
            k = owner * rel_dev + which
            total = None
            for x_ref, g_ref, st, ct in ((x0, g0, st0, ct0), (x1, g1, st1, ct1)):
                low, skip, count = group_rows(k, st, ct, rows, most)
                mine = (row >= skip) & (row < skip + count)
                g = g_ref[pl.ds(low, most), :]
                term = lax.dot_general(
                    x_ref[pl.ds(low, most), :],
                    jnp.where(mine, g, jnp.zeros_like(g)),
                    (((0,), (0,)), ((), ())),
                    preferred_element_type=f32,
                )
                total = term if total is None else total + term
            total = total.astype(bf16)
            for q in range(n // 2):
                pair = total[2 * q * block : (2 * q + 1) * block], total[(2 * q + 1) * block : (2 * q + 2) * block]
                keep = jnp.where(second, pair[1], pair[0])
                send = jnp.where(second, pair[0], pair[1])
                for c in range(2):
                    columns = slice(c * wide, (c + 1) * wide)
                    keep_ref[c, slot_ref[c, q], away_ref[owner]] = keep[:, columns]
                    send_ref[c, slot_ref[c, q], away_ref[owner]] = send[:, columns]

    half = jax.ShapeDtypeStruct((2, n // 2, m, block, wide), bf16)
    return call(
        kernel,
        (half, half),
        [smem()] * 7 + [vmem()] * 4,
        (),
        4 * m * most * width * width,
        0,
    )(core, slot, away, starts[0], counts[0], starts[1], counts[1], *xs, *gs)


def add(a, b):
    return (a.astype(f32) + b.astype(f32)).astype(bf16)


def add_halves(mine, came):
    half = mine.shape[0] // 2
    return add(mine[:half], came[:half]), add(mine[half:], came[half:])


def sort_places(rel_ids, nrel):
    ids = rel_ids[:, 0]
    rows = ids.shape[0]
    onehot = ids[None, :] == jnp.arange(nrel, dtype=jnp.int32)[:, None]
    lanes = 128
    blocks = onehot.astype(bf16).reshape(nrel, rows // lanes, lanes)
    upto = (jnp.arange(lanes)[:, None] <= jnp.arange(lanes)[None, :]).astype(bf16)
    within = lax.dot_general(
        blocks, upto, (((2,), (0,)), ((), ())), preferred_element_type=f32
    )
    sums = within[:, :, -1]
    before = jnp.cumsum(sums, axis=1) - sums
    counts = jnp.sum(sums, axis=1).astype(jnp.int32)
    padded = (counts + ALIGN - 1) // ALIGN * ALIGN
    starts = jnp.cumsum(padded) - padded
    rank = (within + before[:, :, None]).reshape(nrel, rows).astype(jnp.int32) - 1
    place = jnp.sum(jnp.where(onehot, rank + starts[:, None], 0), axis=0)
    return place, starts.astype(jnp.int32), counts


def places_of(place, rows):
    return (jnp.arange(rows, dtype=jnp.int32)[:, None] == place[None, :]).astype(bf16)


def sample_fields(picks, target, stop, part_rows):
    groups, bits = part_rows // FIELDS, picks.shape[0].bit_length()
    picks = picks.astype(jnp.int32) - 1
    target = target.astype(jnp.int32)
    held = jnp.where(picks >= 0, jnp.left_shift(1, bits * (jnp.maximum(picks, 0) // groups)), 0)
    row = jnp.maximum(target[1:2] - 1, 0)
    field = row // groups
    flag = jnp.left_shift(1, bits * field) + jnp.left_shift(1, bits * FIELDS + field)
    group = jnp.concatenate([jnp.maximum(picks, 0), row], 0) % groups
    addend = jnp.concatenate([held, jnp.where(target[0:1] == stop + 1, flag, 0)], 0)
    return group.astype(jnp.int32), addend.astype(jnp.int32)


def coefficients(group, addend, part_rows):
    entries, rows = group.shape
    groups, bits = part_rows // FIELDS, (entries - 1).bit_length()
    lanes = 128

    def kernel(group_ref, addend_ref, plus_ref, minus_ref):
        mine = lax.broadcasted_iota(jnp.int32, (groups, lanes), 0)
        for left in range(0, rows, lanes):
            cols = slice(left, left + lanes)
            packed = jnp.zeros((groups, lanes), jnp.int32)
            for k in range(entries):
                packed = packed + jnp.where(
                    mine == group_ref[k : k + 1, cols], addend_ref[k : k + 1, cols], 0
                )
            for f in range(FIELDS):
                both = ((packed >> (bits * f)) & ((1 << bits) - 1)).astype(f32) * 0.5
                hit = ((packed >> (bits * FIELDS + f)) & 1).astype(f32)
                plus_ref[f * groups : (f + 1) * groups, cols] = both.astype(bf16)
                minus_ref[f * groups : (f + 1) * groups, cols] = (both - hit).astype(bf16)

    shape = jax.ShapeDtypeStruct((part_rows, rows), bf16)
    return call(
        kernel, (shape, shape), [vmem()] * 2, (), 10**9, 4 * part_rows * rows
    )(group, addend)


def shards(source_rows, rel_ids, relations, entities, pos_slot, negatives):
    src_rows, width = source_rows.shape
    rel_dev = relations.shape[0]
    n, m = lax.axis_size("cand"), lax.axis_size("rel")
    nrel = rel_dev * m
    stops, _, samples = negatives.shape
    part_rows = entities.shape[0]
    rows = src_rows + nrel * ALIGN
    odd = lax.axis_index("cand") % 2 == 1

    held = gather_start(relations)

    place, starts, counts = sort_places(rel_ids, nrel)
    onto = places_of(place, rows)
    listed = (jnp.swapaxes(negatives, 1, 2) + 1).reshape(stops * samples, src_rows)
    wanted = jnp.stack([pos_slot // part_rows + 1, pos_slot % part_rows + 1])
    listed = jnp.concatenate([listed, wanted], 0).astype(bf16)
    listed = lax.dot_general(
        listed, onto, (((1,), (1,)), ((), ())), preferred_element_type=f32
    ).astype(bf16)
    listed = jnp.concatenate(
        [listed[:-2].reshape(stops, samples, rows)[i::2].reshape(-1, rows) for i in range(2)] + [listed[-2:]], 0
    )
    even = (stops + 1) // 2 * samples
    listed_own = jnp.concatenate([listed[:even], listed[-2:]], 0)
    listed_sib = swap(listed[even:], 1)

    spans = swap(jnp.stack([starts, counts]), 1)
    starts_sib, counts_sib = spans[0], spans[1]

    held[0], listed_own, listed_sib = lax.optimization_barrier((held[0], listed_own, listed_sib))
    picks = (listed_own[:-2].reshape(-1, samples, rows), listed_sib[:-2].reshape(-1, samples, rows))
    targets = (listed_own[-2:], listed_sib[-2:])
    made = {}

    def prepare(stop, after):
        if stop < stops:
            group, addend = sample_fields(picks[stop % 2][stop // 2], targets[stop % 2], stop, part_rows)
            group, addend, _ = lax.optimization_barrier((group, addend, after))
            made[stop] = coefficients(group, addend, part_rows)

    steps = len(chip_bits())
    for step in range(steps):
        held = gather_step(held, step)
        if step == 0:
            held[0], held[1], source_rows = lax.optimization_barrier((held[0], held[1], source_rows))
            x_own = jnp.dot(onto, source_rows, preferred_element_type=f32).astype(bf16)
            x_sib = swap(x_own, 1)
            prepare(0, held[0])
    near = jnp.stack(held)
    first = entities.astype(bf16)
    near, x_own, first, made[0] = lax.optimization_barrier((near, x_own, first, made[0]))
    prepare(1, near)
    far = swap(near, 1)
    far, made[1] = lax.optimization_barrier((far, made[1]))
    q_own = project(x_own, starts, counts, relations, near, far, False, True)
    q_sib = project(x_sib, starts_sib, counts_sib, relations, near, far, False, True)

    state = entities
    parts = [[], []]
    acc = [None, None]
    for stop in range(stops):
        mine = stop % 2
        queries = (q_own, q_sib)[mine]
        plus, minus = made[stop]
        wide = state.astype(bf16) if stop else first
        logits = lax.dot_general(
            wide, queries, (((1,), (1,)), ((), ())), preferred_element_type=f32
        )
        weight = (
            plus.astype(f32) * jnp.tanh(0.5 * logits) + minus.astype(f32)
        ).astype(bf16)
        for ahead in (1, 2) if stop == stops - 3 else (1,) if 0 < stop < stops - 2 else ():
            prepare(stop + ahead, weight)
        state = state - learn_rate * jnp.dot(weight, queries, preferred_element_type=f32)
        if stop + 1 < stops:
            moving = 1 - mine
            route = [(i, (i + 2) % n) for i in range(n) if i % 2 == moving]
            came = lax.ppermute(state.astype(bf16), "cand", route)
        parts[mine].append((weight, wide))
        if stop == 2:
            nothing = weight[0, 0] * 0
            x_own, x_sib = x_own + nothing, x_sib + nothing
        if stop >= stops - 4:
            together = list(zip(*parts[mine]))
            part = lax.dot_general(
                jnp.concatenate(together[0], 0),
                jnp.concatenate(together[1], 0),
                (((0,), (0,)), ((), ())),
                preferred_element_type=f32,
            )
            acc[mine] = part if acc[mine] is None else (acc[mine] + part).astype(bf16)
            parts[mine] = []
            if stop + 1 < stops:
                came, acc[mine] = lax.optimization_barrier((came, acc[mine]))
        if stop == 0:
            came, q_sib = lax.optimization_barrier((came, q_sib))
        if stop + 1 < stops:
            state = jnp.where(odd == (moving == 1), came.astype(f32), state)

    g_own, g_sib = acc
    raw = [
        relation_terms((x_own, x_sib), (g_own, g_sib), (starts, starts_sib), (counts, counts_sib), rel_dev, which)
        for which in range(rel_dev)
    ]
    came = [swap(send, 1) for _, send in raw]
    for i in range(rel_dev - 1):
        came[i], *raw[i + 1] = lax.optimization_barrier((came[i], *raw[i + 1]))
    waves = [[add_halves(keep[c], other[c]) for c in range(2)] for (keep, _), other in zip(raw, came)]
    begun = [part[1] for wave in waves for part in wave]
    query_grad = add(g_own, swap(g_sib, 1))
    query_grad, state, _ = lax.optimization_barrier((query_grad, state, begun))
    back = project(query_grad, starts, counts, relations, near, far, True, False)
    for step in range(steps):
        came = [[swap(part[1], order[step]) for part, order in zip(wave, bit_orders())] for wave in waves]
        if step == 0:
            came, back = lax.optimization_barrier((came, back))
        if step + 1 < steps:
            waves = [[add_halves(part[0], c) for part, c in zip(*both)] for both in zip(waves, came)]
    pairs = []
    for wave, other in zip(waves, came):
        parts = [add_halves(part[0][0], c[0]) for part, c in zip(wave, other)]
        pairs.append([jnp.concatenate(both, -1) for both in zip(*parts)])
    source_grad = []
    for i, bit in enumerate(rel_bits()):
        came = [swap_rel(send, bit) for _, send in pairs]
        if i < 2:
            sorted_rows, _ = lax.optimization_barrier((back, [send for _, send in pairs]))
            source_grad.append(
                lax.dot_general(
                    places_of(place[i * src_rows // 2 : (i + 1) * src_rows // 2], rows),
                    sorted_rows,
                    (((0,), (0,)), ((), ())),
                    preferred_element_type=f32,
                ).astype(bf16)
            )
            came, source_grad[i] = lax.optimization_barrier((came, source_grad[i]))
        if pairs[0][0].shape[0] > 1:
            pairs = [add_halves(keep, other) for (keep, _), other in zip(pairs, came)]
    relation_grad = jnp.stack(
        [keep[0].astype(f32) + other[0].astype(f32) for (keep, _), other in zip(pairs, came)], 1
    )
    source_grad = jnp.concatenate(source_grad, 0)
    updated = swap(state, 1) if stops % 2 == 0 else state
    return updated, source_grad, relation_grad


def solution(mesh):
    placed = (
        P(("cand", "rel"), None),
        P(("cand", "rel"), None),
        P("rel", None, None),
        P(("cand", "rel"), None),
        P(("cand", "rel")),
        P(None, ("cand", "rel"), None),
    )
    return jax.shard_map(
        shards,
        mesh=mesh,
        in_specs=placed,
        out_specs=(P(("cand", "rel"), None), P(("cand", "rel"), None), P("cand", "rel", None)),
        check_vma=False,
    )
```

```python
import jax
import jax.numpy as jnp
from jax import lax
from jax.experimental import pallas as pl
from jax.experimental.pallas import tpu as pltpu
from jax.sharding import PartitionSpec as P

learn_rate = 0.005
ALIGN = 16
FIELDS = 4
bf16 = jnp.bfloat16
f32 = jnp.float32
VMEM_LIMIT = 14 * 2**20


def swap(x, bit):
    return lax.ppermute(x, "cand", [(i, i ^ bit) for i in range(lax.axis_size("cand"))])


def swap_rel(x, bit):
    return lax.ppermute(x, "rel", [(i, i ^ bit) for i in range(lax.axis_size("rel"))])


def rel_bits():
    return [1 << i for i in range((lax.axis_size("rel") - 1).bit_length())]


def chip_bits():
    bits, bit = [], 2
    while bit < lax.axis_size("cand"):
        bits.append(bit)
        bit *= 2
    return bits


def bit_orders():
    bits = chip_bits()
    return bits, bits[::-1]


def vmem():
    return pl.BlockSpec(memory_space=pltpu.VMEM)


def smem():
    return pl.BlockSpec(memory_space=pltpu.SMEM)


def anywhere():
    return pl.BlockSpec(memory_space=pl.ANY)


def call(kernel, out_shape, in_specs, scratch=(), flops=0, moved=0):
    return pl.pallas_call(
        kernel,
        out_shape=out_shape,
        in_specs=in_specs,
        out_specs=jax.tree.map(lambda _: vmem(), out_shape),
        scratch_shapes=scratch,
        compiler_params=pltpu.CompilerParams(vmem_limit_bytes=VMEM_LIMIT),
        cost_estimate=pl.CostEstimate(flops=flops, bytes_accessed=moved, transcendentals=0),
    )


def gather_start(relations):
    n, m = lax.axis_size("cand"), lax.axis_size("rel")
    width = relations.shape[-1]
    flat = relations.reshape(-1, width)
    piece = flat.shape[0] // n
    own = lax.dynamic_slice(flat, (lax.axis_index("cand") * piece, 0), (piece, width))
    came = jnp.stack([swap_rel(own, j) for j in range(1, m)])
    half = piece // 2
    return [came[None, :, h * half : (h + 1) * half] for h in range(2)]


def gather_step(held, step):
    return [
        jnp.concatenate([part, swap(part, order[step])], 0) for part, order in zip(held, bit_orders())
    ]


def piece_slots():
    n = lax.axis_size("cand")
    apart = jnp.arange(n, dtype=jnp.int32) ^ lax.axis_index("cand")
    tables = []
    for order in bit_orders():
        slot = jnp.zeros_like(apart)
        for place, bit in enumerate(order):
            slot = slot + jnp.where((apart & bit) != 0, 1 << place, 0)
        tables.append(slot)
    return jnp.stack(tables + [apart & 1]).astype(jnp.int32)


def group_rows(k, starts, counts, rows, most):
    first = starts[k]
    low = pl.multiple_of(jnp.minimum(first, rows - most), ALIGN)
    return low, first - low, counts[k]


def project(x, starts, counts, relations, near, far, transposed, fresh):
    m = lax.axis_size("rel")
    rel_dev = relations.shape[0]
    nrel = rel_dev * m
    rows, width = x.shape
    most = 2 * (rows - nrel * ALIGN) // nrel
    half = near.shape[3]
    per = width // (2 * half)
    dims = (((1,), (1 if transposed else 0,)), ((), ()))
    me = lax.axis_index("rel").astype(jnp.int32).reshape(1)

    def kernel(me_ref, slots, starts_ref, counts_ref, *rest):
        given, out_ref, held = rest[:4], rest[4], rest[5:]
        copies = []
        if not fresh:
            copies = [pltpu.make_async_copy(given[i], held[i], held[4].at[i]) for i in range(4)]
        for copy in copies:
            copy.start()
        x_ref, rel_ref, near_ref, far_ref = given if fresh else held[:4]
        out_ref[...] = jnp.zeros_like(out_ref)
        for copy in copies[:2]:
            copy.wait()
        row = lax.broadcasted_iota(jnp.int32, (most, 1), 0)
        for away in range(m):
            if away == 1:
                for copy in copies[2:]:
                    copy.wait()
            for which in range(rel_dev):
                if away == 0:
                    matrix = rel_ref[which]
                else:
                    parts = []
                    for c in range(which * per, which * per + per):
                        for h in range(2):
                            at = slots[h, c]
                            parts.append(
                                jnp.where(slots[2, c] == 1, far_ref[h, at, away - 1], near_ref[h, at, away - 1])
                            )
                    matrix = jnp.concatenate(parts, 0)
                k = (me_ref[0] ^ away) * rel_dev + which
                low, skip, count = group_rows(k, starts_ref, counts_ref, rows, most)
                got = lax.dot_general(
                    x_ref[pl.ds(low, most), :], matrix, dims, preferred_element_type=f32
                ).astype(bf16)
                mine = (row >= skip) & (row < skip + count)
                out_ref[pl.ds(low, most), :] = jnp.where(mine, got, out_ref[pl.ds(low, most), :])

    return pl.pallas_call(
        kernel,
        out_shape=jax.ShapeDtypeStruct((rows, width), bf16),
        in_specs=[smem()] * 4 + [vmem() if fresh else anywhere()] * 4,
        out_specs=vmem(),
        scratch_shapes=[]
        if fresh
        else [
            pltpu.VMEM(x.shape, bf16),
            pltpu.VMEM(relations.shape, bf16),
            pltpu.VMEM(near.shape, bf16),
            pltpu.VMEM(far.shape, bf16),
            pltpu.SemaphoreType.DMA((4,)),
        ],
        compiler_params=pltpu.CompilerParams(vmem_limit_bytes=(13 if fresh else 60) * 2**20),
        cost_estimate=pl.CostEstimate(
            flops=2 * nrel * most * width * width, bytes_accessed=8 * 2**20, transcendentals=0
        ),
    )(me, piece_slots(), starts, counts, x, relations, near, far)


def far_first(apart, bits):
    place = jnp.zeros_like(apart)
    for i, bit in enumerate(bits):
        place = place + jnp.where((apart & bit) != 0, 1 << (len(bits) - 1 - i), 0)
    return place.astype(jnp.int32)


def relation_terms(xs, gs, starts, counts, rel_dev, which):
    n, m = lax.axis_size("cand"), lax.axis_size("rel")
    nrel = rel_dev * m
    rows, width = xs[0].shape
    most = 2 * (rows - nrel * ALIGN) // nrel
    block, wide = width // n, width // 2
    me = lax.axis_index("cand")
    apart = (jnp.arange(n // 2, dtype=jnp.int32) ^ (me // 2)) * 2
    slot = jnp.stack([far_first(apart, order) for order in bit_orders()])
    away = far_first(jnp.arange(m, dtype=jnp.int32) ^ lax.axis_index("rel"), rel_bits())
    core = (me % 2).astype(jnp.int32).reshape(1)

    def kernel(core_ref, slot_ref, away_ref, st0, ct0, st1, ct1, x0, x1, g0, g1, keep_ref, send_ref):
        row = lax.broadcasted_iota(jnp.int32, (most, 1), 0)
        second = core_ref[0] == 1
        for owner in range(m):
            k = owner * rel_dev + which
            total = None
            for x_ref, g_ref, st, ct in ((x0, g0, st0, ct0), (x1, g1, st1, ct1)):
                low, skip, count = group_rows(k, st, ct, rows, most)
                mine = (row >= skip) & (row < skip + count)
                g = g_ref[pl.ds(low, most), :]
                term = lax.dot_general(
                    x_ref[pl.ds(low, most), :],
                    jnp.where(mine, g, jnp.zeros_like(g)),
                    (((0,), (0,)), ((), ())),
                    preferred_element_type=f32,
                )
                total = term if total is None else total + term
            total = total.astype(bf16)
            for q in range(n // 2):
                pair = total[2 * q * block : (2 * q + 1) * block], total[(2 * q + 1) * block : (2 * q + 2) * block]
                keep = jnp.where(second, pair[1], pair[0])
                send = jnp.where(second, pair[0], pair[1])
                for c in range(2):
                    columns = slice(c * wide, (c + 1) * wide)
                    keep_ref[c, slot_ref[c, q], away_ref[owner]] = keep[:, columns]
                    send_ref[c, slot_ref[c, q], away_ref[owner]] = send[:, columns]

    half = jax.ShapeDtypeStruct((2, n // 2, m, block, wide), bf16)
    return call(
        kernel,
        (half, half),
        [smem()] * 7 + [vmem()] * 4,
        (),
        4 * m * most * width * width,
        0,
    )(core, slot, away, starts[0], counts[0], starts[1], counts[1], *xs, *gs)


def add(a, b):
    return (a.astype(f32) + b.astype(f32)).astype(bf16)


def add_halves(mine, came):
    half = mine.shape[0] // 2
    return add(mine[:half], came[:half]), add(mine[half:], came[half:])


def sort_places(rel_ids, nrel):
    ids = rel_ids[:, 0]
    rows = ids.shape[0]
    onehot = ids[None, :] == jnp.arange(nrel, dtype=jnp.int32)[:, None]
    lanes = 128
    blocks = onehot.astype(bf16).reshape(nrel, rows // lanes, lanes)
    upto = (jnp.arange(lanes)[:, None] <= jnp.arange(lanes)[None, :]).astype(bf16)
    within = lax.dot_general(
        blocks, upto, (((2,), (0,)), ((), ())), preferred_element_type=f32
    )
    sums = within[:, :, -1]
    before = jnp.cumsum(sums, axis=1) - sums
    counts = jnp.sum(sums, axis=1).astype(jnp.int32)
    padded = (counts + ALIGN - 1) // ALIGN * ALIGN
    starts = jnp.cumsum(padded) - padded
    rank = (within + before[:, :, None]).reshape(nrel, rows).astype(jnp.int32) - 1
    place = jnp.sum(jnp.where(onehot, rank + starts[:, None], 0), axis=0)
    return place, starts.astype(jnp.int32), counts


def places_of(place, rows):
    return (jnp.arange(rows, dtype=jnp.int32)[:, None] == place[None, :]).astype(bf16)


def sample_fields(picks, target, stop, part_rows):
    groups, bits = part_rows // FIELDS, picks.shape[0].bit_length()
    picks = picks.astype(jnp.int32) - 1
    target = target.astype(jnp.int32)
    held = jnp.where(picks >= 0, jnp.left_shift(1, bits * (jnp.maximum(picks, 0) // groups)), 0)
    row = jnp.maximum(target[1:2] - 1, 0)
    field = row // groups
    flag = jnp.left_shift(1, bits * field) + jnp.left_shift(1, bits * FIELDS + field)
    group = jnp.concatenate([jnp.maximum(picks, 0), row], 0) % groups
    addend = jnp.concatenate([held, jnp.where(target[0:1] == stop + 1, flag, 0)], 0)
    return group.astype(jnp.int32), addend.astype(jnp.int32)


def coefficients(group, addend, part_rows):
    entries, rows = group.shape
    groups, bits = part_rows // FIELDS, (entries - 1).bit_length()
    lanes = 128

    def kernel(group_ref, addend_ref, plus_ref, minus_ref):
        mine = lax.broadcasted_iota(jnp.int32, (groups, lanes), 0)
        for left in range(0, rows, lanes):
            cols = slice(left, left + lanes)
            packed = jnp.zeros((groups, lanes), jnp.int32)
            for k in range(entries):
                packed = packed + jnp.where(
                    mine == group_ref[k : k + 1, cols], addend_ref[k : k + 1, cols], 0
                )
            for f in range(FIELDS):
                both = ((packed >> (bits * f)) & ((1 << bits) - 1)).astype(f32) * 0.5
                hit = ((packed >> (bits * FIELDS + f)) & 1).astype(f32)
                plus_ref[f * groups : (f + 1) * groups, cols] = both.astype(bf16)
                minus_ref[f * groups : (f + 1) * groups, cols] = (both - hit).astype(bf16)

    shape = jax.ShapeDtypeStruct((part_rows, rows), bf16)
    return call(
        kernel, (shape, shape), [vmem()] * 2, (), 10**9, 4 * part_rows * rows
    )(group, addend)


def shards(source_rows, rel_ids, relations, entities, pos_slot, negatives):
    src_rows, width = source_rows.shape
    rel_dev = relations.shape[0]
    n, m = lax.axis_size("cand"), lax.axis_size("rel")
    nrel = rel_dev * m
    stops, _, samples = negatives.shape
    part_rows = entities.shape[0]
    rows = src_rows + nrel * ALIGN
    odd = lax.axis_index("cand") % 2 == 1

    held = gather_start(relations)

    place, starts, counts = sort_places(rel_ids, nrel)
    onto = places_of(place, rows)
    listed = (jnp.swapaxes(negatives, 1, 2) + 1).reshape(stops * samples, src_rows)
    wanted = jnp.stack([pos_slot // part_rows + 1, pos_slot % part_rows + 1])
    listed = jnp.concatenate([listed, wanted], 0).astype(bf16)
    listed = lax.dot_general(
        listed, onto, (((1,), (1,)), ((), ())), preferred_element_type=f32
    ).astype(bf16)
    listed = jnp.concatenate(
        [listed[:-2].reshape(stops, samples, rows)[i::2].reshape(-1, rows) for i in range(2)] + [listed[-2:]], 0
    )
    even = (stops + 1) // 2 * samples
    listed_own = jnp.concatenate([listed[:even], listed[-2:]], 0)
    listed_sib = swap(listed[even:], 1)

    spans = swap(jnp.stack([starts, counts]), 1)
    starts_sib, counts_sib = spans[0], spans[1]

    held[0], listed_own, listed_sib = lax.optimization_barrier((held[0], listed_own, listed_sib))
    picks = (listed_own[:-2].reshape(-1, samples, rows), listed_sib[:-2].reshape(-1, samples, rows))
    targets = (listed_own[-2:], listed_sib[-2:])
    made = {}

    def prepare(stop, after):
        if stop < stops:
            group, addend = sample_fields(picks[stop % 2][stop // 2], targets[stop % 2], stop, part_rows)
            group, addend, _ = lax.optimization_barrier((group, addend, after))
            made[stop] = coefficients(group, addend, part_rows)

    steps = len(chip_bits())
    for step in range(steps):
        held = gather_step(held, step)
        if step == 0:
            held[0], held[1], source_rows = lax.optimization_barrier((held[0], held[1], source_rows))
            x_own = jnp.dot(onto, source_rows, preferred_element_type=f32).astype(bf16)
            x_sib = swap(x_own, 1)
            prepare(0, held[0])
    near = jnp.stack(held)
    first = entities.astype(bf16)
    near, x_own, first, made[0] = lax.optimization_barrier((near, x_own, first, made[0]))
    prepare(1, near)
    far = swap(near, 1)
    far, made[1] = lax.optimization_barrier((far, made[1]))
    q_own = project(x_own, starts, counts, relations, near, far, False, True)
    q_sib = project(x_sib, starts_sib, counts_sib, relations, near, far, False, True)

    state = entities
    parts = [[], []]
    acc = [None, None]
    for stop in range(stops):
        mine = stop % 2
        queries = (q_own, q_sib)[mine]
        plus, minus = made[stop]
        wide = state.astype(bf16) if stop else first
        logits = lax.dot_general(
            wide, queries, (((1,), (1,)), ((), ())), preferred_element_type=f32
        )
        weight = (
            plus.astype(f32) * jnp.tanh(0.5 * logits) + minus.astype(f32)
        ).astype(bf16)
        for ahead in (1, 2) if stop == stops - 3 else (1,) if 0 < stop < stops - 2 else ():
            prepare(stop + ahead, weight)
        state = state - learn_rate * jnp.dot(weight, queries, preferred_element_type=f32)
        if stop + 1 < stops:
            moving = 1 - mine
            route = [(i, (i + 2) % n) for i in range(n) if i % 2 == moving]
            came = lax.ppermute(state.astype(bf16), "cand", route)
        parts[mine].append((weight, wide))
        if stop == 2:
            nothing = weight[0, 0] * 0
            x_own, x_sib = x_own + nothing, x_sib + nothing
        if stop >= stops - 4:
            together = list(zip(*parts[mine]))
            part = lax.dot_general(
                jnp.concatenate(together[0], 0),
                jnp.concatenate(together[1], 0),
                (((0,), (0,)), ((), ())),
                preferred_element_type=f32,
            )
            acc[mine] = part if acc[mine] is None else (acc[mine] + part).astype(bf16)
            parts[mine] = []
            if stop + 1 < stops:
                came, acc[mine] = lax.optimization_barrier((came, acc[mine]))
        if stop == 0:
            came, q_sib = lax.optimization_barrier((came, q_sib))
        if stop + 1 < stops:
            state = jnp.where(odd == (moving == 1), came.astype(f32), state)

    g_own, g_sib = acc
    raw = [
        relation_terms((x_own, x_sib), (g_own, g_sib), (starts, starts_sib), (counts, counts_sib), rel_dev, which)
        for which in range(rel_dev)
    ]
    came = [swap(send, 1) for _, send in raw]
    for i in range(rel_dev - 1):
        came[i], *raw[i + 1] = lax.optimization_barrier((came[i], *raw[i + 1]))
    waves = [[add_halves(keep[c], other[c]) for c in range(2)] for (keep, _), other in zip(raw, came)]
    begun = [part[1] for wave in waves for part in wave]
    query_grad = add(g_own, swap(g_sib, 1))
    query_grad, state, _ = lax.optimization_barrier((query_grad, state, begun))
    back = project(query_grad, starts, counts, relations, near, far, True, False)
    for step in range(steps):
        came = [[swap(part[1], order[step]) for part, order in zip(wave, bit_orders())] for wave in waves]
        if step == 0:
            came, back = lax.optimization_barrier((came, back))
        if step + 1 < steps:
            waves = [[add_halves(part[0], c) for part, c in zip(*both)] for both in zip(waves, came)]
    pairs = []
    for wave, other in zip(waves, came):
        parts = [add_halves(part[0][0], c[0]) for part, c in zip(wave, other)]
        pairs.append([jnp.concatenate(both, -1) for both in zip(*parts)])
    source_grad = []
    for i, bit in enumerate(rel_bits()):
        came = [swap_rel(send, bit) for _, send in pairs]
        if i < 2:
            sorted_rows, _ = lax.optimization_barrier((back, [send for _, send in pairs]))
            source_grad.append(
                lax.dot_general(
                    places_of(place[i * src_rows // 2 : (i + 1) * src_rows // 2], rows),
                    sorted_rows,
                    (((0,), (0,)), ((), ())),
                    preferred_element_type=f32,
                ).astype(bf16)
            )
            came, source_grad[i] = lax.optimization_barrier((came, source_grad[i]))
        if pairs[0][0].shape[0] > 1:
            pairs = [add_halves(keep, other) for (keep, _), other in zip(pairs, came)]
    relation_grad = jnp.stack(
        [keep[0].astype(f32) + other[0].astype(f32) for (keep, _), other in zip(pairs, came)], 1
    )
    source_grad = jnp.concatenate(source_grad, 0)
    updated = swap(state, 1) if stops % 2 == 0 else state
    return updated, source_grad, relation_grad


def solution(mesh):
    placed = (
        P(("cand", "rel"), None),
        P(("cand", "rel"), None),
        P("rel", None, None),
        P(("cand", "rel"), None),
        P(("cand", "rel")),
        P(None, ("cand", "rel"), None),
    )
    return jax.shard_map(
        shards,
        mesh=mesh,
        in_specs=placed,
        out_specs=(P(("cand", "rel"), None), P(("cand", "rel"), None), P("cand", "rel", None)),
        check_vma=False,
    )
```

```python
import jax
import jax.numpy as jnp
from jax import lax
from jax.experimental import pallas as pl
from jax.experimental.pallas import tpu as pltpu
from jax.sharding import PartitionSpec as P

learn_rate = 0.005
ALIGN = 16
FIELDS = 4
bf16 = jnp.bfloat16
f32 = jnp.float32
VMEM_LIMIT = 14 * 2**20


def swap(x, bit):
    return lax.ppermute(x, "cand", [(i, i ^ bit) for i in range(lax.axis_size("cand"))])


def swap_rel(x, bit):
    return lax.ppermute(x, "rel", [(i, i ^ bit) for i in range(lax.axis_size("rel"))])


def rel_bits():
    return [1 << i for i in range((lax.axis_size("rel") - 1).bit_length())]


def chip_bits():
    bits, bit = [], 2
    while bit < lax.axis_size("cand"):
        bits.append(bit)
        bit *= 2
    return bits


def bit_orders():
    bits = chip_bits()
    return bits, bits[::-1]


def vmem():
    return pl.BlockSpec(memory_space=pltpu.VMEM)


def smem():
    return pl.BlockSpec(memory_space=pltpu.SMEM)


def anywhere():
    return pl.BlockSpec(memory_space=pl.ANY)


def call(kernel, out_shape, in_specs, scratch=(), flops=0, moved=0):
    return pl.pallas_call(
        kernel,
        out_shape=out_shape,
        in_specs=in_specs,
        out_specs=jax.tree.map(lambda _: vmem(), out_shape),
        scratch_shapes=scratch,
        compiler_params=pltpu.CompilerParams(vmem_limit_bytes=VMEM_LIMIT),
        cost_estimate=pl.CostEstimate(flops=flops, bytes_accessed=moved, transcendentals=0),
    )


def gather_start(relations):
    n, m = lax.axis_size("cand"), lax.axis_size("rel")
    width = relations.shape[-1]
    flat = relations.reshape(-1, width)
    piece = flat.shape[0] // n
    own = lax.dynamic_slice(flat, (lax.axis_index("cand") * piece, 0), (piece, width))
    came = jnp.stack([swap_rel(own, j) for j in range(1, m)])
    half = piece // 2
    return [came[None, :, h * half : (h + 1) * half] for h in range(2)]


def gather_step(held, step):
    return [
        jnp.concatenate([part, swap(part, order[step])], 0) for part, order in zip(held, bit_orders())
    ]


def piece_slots():
    n = lax.axis_size("cand")
    apart = jnp.arange(n, dtype=jnp.int32) ^ lax.axis_index("cand")
    tables = []
    for order in bit_orders():
        slot = jnp.zeros_like(apart)
        for place, bit in enumerate(order):
            slot = slot + jnp.where((apart & bit) != 0, 1 << place, 0)
        tables.append(slot)
    return jnp.stack(tables + [apart & 1]).astype(jnp.int32)


def group_rows(k, starts, counts, rows, most):
    first = starts[k]
    low = pl.multiple_of(jnp.minimum(first, rows - most), ALIGN)
    return low, first - low, counts[k]


def project(x, starts, counts, relations, near, far, transposed, fresh):
    m = lax.axis_size("rel")
    rel_dev = relations.shape[0]
    nrel = rel_dev * m
    rows, width = x.shape
    most = 2 * (rows - nrel * ALIGN) // nrel
    half = near.shape[3]
    per = width // (2 * half)
    dims = (((1,), (1 if transposed else 0,)), ((), ()))
    me = lax.axis_index("rel").astype(jnp.int32).reshape(1)

    def kernel(me_ref, slots, starts_ref, counts_ref, *rest):
        given, out_ref, held = rest[:4], rest[4], rest[5:]
        copies = []
        if not fresh:
            copies = [pltpu.make_async_copy(given[i], held[i], held[4].at[i]) for i in range(4)]
        for copy in copies:
            copy.start()
        x_ref, rel_ref, near_ref, far_ref = given if fresh else held[:4]
        out_ref[...] = jnp.zeros_like(out_ref)
        for copy in copies[:2]:
            copy.wait()
        row = lax.broadcasted_iota(jnp.int32, (most, 1), 0)
        for away in range(m):
            if away == 1:
                for copy in copies[2:]:
                    copy.wait()
            for which in range(rel_dev):
                if away == 0:
                    matrix = rel_ref[which]
                else:
                    parts = []
                    for c in range(which * per, which * per + per):
                        for h in range(2):
                            at = slots[h, c]
                            parts.append(
                                jnp.where(slots[2, c] == 1, far_ref[h, at, away - 1], near_ref[h, at, away - 1])
                            )
                    matrix = jnp.concatenate(parts, 0)
                k = (me_ref[0] ^ away) * rel_dev + which
                low, skip, count = group_rows(k, starts_ref, counts_ref, rows, most)
                got = lax.dot_general(
                    x_ref[pl.ds(low, most), :], matrix, dims, preferred_element_type=f32
                ).astype(bf16)
                mine = (row >= skip) & (row < skip + count)
                out_ref[pl.ds(low, most), :] = jnp.where(mine, got, out_ref[pl.ds(low, most), :])

    return pl.pallas_call(
        kernel,
        out_shape=jax.ShapeDtypeStruct((rows, width), bf16),
        in_specs=[smem()] * 4 + [vmem() if fresh else anywhere()] * 4,
        out_specs=vmem(),
        scratch_shapes=[]
        if fresh
        else [
            pltpu.VMEM(x.shape, bf16),
            pltpu.VMEM(relations.shape, bf16),
            pltpu.VMEM(near.shape, bf16),
            pltpu.VMEM(far.shape, bf16),
            pltpu.SemaphoreType.DMA((4,)),
        ],
        compiler_params=pltpu.CompilerParams(vmem_limit_bytes=(13 if fresh else 60) * 2**20),
        cost_estimate=pl.CostEstimate(
            flops=2 * nrel * most * width * width, bytes_accessed=8 * 2**20, transcendentals=0
        ),
    )(me, piece_slots(), starts, counts, x, relations, near, far)


def far_first(apart, bits):
    place = jnp.zeros_like(apart)
    for i, bit in enumerate(bits):
        place = place + jnp.where((apart & bit) != 0, 1 << (len(bits) - 1 - i), 0)
    return place.astype(jnp.int32)


def relation_terms(xs, gs, starts, counts, rel_dev, which):
    n, m = lax.axis_size("cand"), lax.axis_size("rel")
    nrel = rel_dev * m
    rows, width = xs[0].shape
    most = 2 * (rows - nrel * ALIGN) // nrel
    block, wide = width // n, width // 2
    me = lax.axis_index("cand")
    apart = (jnp.arange(n // 2, dtype=jnp.int32) ^ (me // 2)) * 2
    slot = jnp.stack([far_first(apart, order) for order in bit_orders()])
    away = far_first(jnp.arange(m, dtype=jnp.int32) ^ lax.axis_index("rel"), rel_bits())
    core = (me % 2).astype(jnp.int32).reshape(1)

    def kernel(core_ref, slot_ref, away_ref, st0, ct0, st1, ct1, x0, x1, g0, g1, keep_ref, send_ref):
        row = lax.broadcasted_iota(jnp.int32, (most, 1), 0)
        second = core_ref[0] == 1
        for owner in range(m):
            k = owner * rel_dev + which
            total = None
            for x_ref, g_ref, st, ct in ((x0, g0, st0, ct0), (x1, g1, st1, ct1)):
                low, skip, count = group_rows(k, st, ct, rows, most)
                mine = (row >= skip) & (row < skip + count)
                g = g_ref[pl.ds(low, most), :]
                term = lax.dot_general(
                    x_ref[pl.ds(low, most), :],
                    jnp.where(mine, g, jnp.zeros_like(g)),
                    (((0,), (0,)), ((), ())),
                    preferred_element_type=f32,
                )
                total = term if total is None else total + term
            total = total.astype(bf16)
            for q in range(n // 2):
                pair = total[2 * q * block : (2 * q + 1) * block], total[(2 * q + 1) * block : (2 * q + 2) * block]
                keep = jnp.where(second, pair[1], pair[0])
                send = jnp.where(second, pair[0], pair[1])
                for c in range(2):
                    columns = slice(c * wide, (c + 1) * wide)
                    keep_ref[c, slot_ref[c, q], away_ref[owner]] = keep[:, columns]
                    send_ref[c, slot_ref[c, q], away_ref[owner]] = send[:, columns]

    half = jax.ShapeDtypeStruct((2, n // 2, m, block, wide), bf16)
    return call(
        kernel,
        (half, half),
        [smem()] * 7 + [vmem()] * 4,
        (),
        4 * m * most * width * width,
        0,
    )(core, slot, away, starts[0], counts[0], starts[1], counts[1], *xs, *gs)


def add(a, b):
    return (a.astype(f32) + b.astype(f32)).astype(bf16)


def add_halves(mine, came):
    half = mine.shape[0] // 2
    return add(mine[:half], came[:half]), add(mine[half:], came[half:])


def sort_places(rel_ids, nrel):
    ids = rel_ids[:, 0]
    rows = ids.shape[0]
    onehot = ids[None, :] == jnp.arange(nrel, dtype=jnp.int32)[:, None]
    lanes = 128
    blocks = onehot.astype(bf16).reshape(nrel, rows // lanes, lanes)
    upto = (jnp.arange(lanes)[:, None] <= jnp.arange(lanes)[None, :]).astype(bf16)
    within = lax.dot_general(
        blocks, upto, (((2,), (0,)), ((), ())), preferred_element_type=f32
    )
    sums = within[:, :, -1]
    before = jnp.cumsum(sums, axis=1) - sums
    counts = jnp.sum(sums, axis=1).astype(jnp.int32)
    padded = (counts + ALIGN - 1) // ALIGN * ALIGN
    starts = jnp.cumsum(padded) - padded
    rank = (within + before[:, :, None]).reshape(nrel, rows).astype(jnp.int32) - 1
    place = jnp.sum(jnp.where(onehot, rank + starts[:, None], 0), axis=0)
    return place, starts.astype(jnp.int32), counts


def places_of(place, rows):
    return (jnp.arange(rows, dtype=jnp.int32)[:, None] == place[None, :]).astype(bf16)


def sample_fields(picks, target, stop, part_rows):
    groups, bits = part_rows // FIELDS, picks.shape[0].bit_length()
    picks = picks.astype(jnp.int32) - 1
    target = target.astype(jnp.int32)
    held = jnp.where(picks >= 0, jnp.left_shift(1, bits * (jnp.maximum(picks, 0) // groups)), 0)
    row = jnp.maximum(target[1:2] - 1, 0)
    field = row // groups
    flag = jnp.left_shift(1, bits * field) + jnp.left_shift(1, bits * FIELDS + field)
    group = jnp.concatenate([jnp.maximum(picks, 0), row], 0) % groups
    addend = jnp.concatenate([held, jnp.where(target[0:1] == stop + 1, flag, 0)], 0)
    return group.astype(jnp.int32), addend.astype(jnp.int32)


def coefficients(group, addend, part_rows):
    entries, rows = group.shape
    groups, bits = part_rows // FIELDS, (entries - 1).bit_length()
    lanes = 128

    def kernel(group_ref, addend_ref, plus_ref, minus_ref):
        mine = lax.broadcasted_iota(jnp.int32, (groups, lanes), 0)
        for left in range(0, rows, lanes):
            cols = slice(left, left + lanes)
            packed = jnp.zeros((groups, lanes), jnp.int32)
            for k in range(entries):
                packed = packed + jnp.where(
                    mine == group_ref[k : k + 1, cols], addend_ref[k : k + 1, cols], 0
                )
            for f in range(FIELDS):
                both = ((packed >> (bits * f)) & ((1 << bits) - 1)).astype(f32) * 0.5
                hit = ((packed >> (bits * FIELDS + f)) & 1).astype(f32)
                plus_ref[f * groups : (f + 1) * groups, cols] = both.astype(bf16)
                minus_ref[f * groups : (f + 1) * groups, cols] = (both - hit).astype(bf16)

    shape = jax.ShapeDtypeStruct((part_rows, rows), bf16)
    return call(
        kernel, (shape, shape), [vmem()] * 2, (), 10**9, 4 * part_rows * rows
    )(group, addend)


def shards(source_rows, rel_ids, relations, entities, pos_slot, negatives):
    src_rows, width = source_rows.shape
    rel_dev = relations.shape[0]
    n, m = lax.axis_size("cand"), lax.axis_size("rel")
    nrel = rel_dev * m
    stops, _, samples = negatives.shape
    part_rows = entities.shape[0]
    rows = src_rows + nrel * ALIGN
    odd = lax.axis_index("cand") % 2 == 1

    held = gather_start(relations)

    place, starts, counts = sort_places(rel_ids, nrel)
    onto = places_of(place, rows)
    listed = (jnp.swapaxes(negatives, 1, 2) + 1).reshape(stops * samples, src_rows)
    wanted = jnp.stack([pos_slot // part_rows + 1, pos_slot % part_rows + 1])
    listed = jnp.concatenate([listed, wanted], 0).astype(bf16)
    listed = lax.dot_general(
        listed, onto, (((1,), (1,)), ((), ())), preferred_element_type=f32
    ).astype(bf16)
    listed = jnp.concatenate(
        [listed[:-2].reshape(stops, samples, rows)[i::2].reshape(-1, rows) for i in range(2)] + [listed[-2:]], 0
    )
    even = (stops + 1) // 2 * samples
    listed_own = jnp.concatenate([listed[:even], listed[-2:]], 0)
    listed_sib = swap(listed[even:], 1)

    spans = swap(jnp.stack([starts, counts]), 1)
    starts_sib, counts_sib = spans[0], spans[1]

    held[0], listed_own, listed_sib = lax.optimization_barrier((held[0], listed_own, listed_sib))
    picks = (listed_own[:-2].reshape(-1, samples, rows), listed_sib[:-2].reshape(-1, samples, rows))
    targets = (listed_own[-2:], listed_sib[-2:])
    made = {}

    def prepare(stop, after):
        if stop < stops:
            group, addend = sample_fields(picks[stop % 2][stop // 2], targets[stop % 2], stop, part_rows)
            group, addend, _ = lax.optimization_barrier((group, addend, after))
            made[stop] = coefficients(group, addend, part_rows)

    steps = len(chip_bits())
    for step in range(steps):
        held = gather_step(held, step)
        if step == 0:
            held[0], held[1], source_rows = lax.optimization_barrier((held[0], held[1], source_rows))
            x_own = jnp.dot(onto, source_rows, preferred_element_type=f32).astype(bf16)
            x_sib = swap(x_own, 1)
            prepare(0, held[0])
    near = jnp.stack(held)
    first = entities.astype(bf16)
    near, x_own, first, made[0] = lax.optimization_barrier((near, x_own, first, made[0]))
    prepare(1, near)
    far = swap(near, 1)
    far, made[1] = lax.optimization_barrier((far, made[1]))
    q_own = project(x_own, starts, counts, relations, near, far, False, True)
    q_sib = project(x_sib, starts_sib, counts_sib, relations, near, far, False, True)

    state = entities
    parts = [[], []]
    acc = [None, None]
    for stop in range(stops):
        mine = stop % 2
        queries = (q_own, q_sib)[mine]
        plus, minus = made[stop]
        wide = state.astype(bf16) if stop else first
        logits = lax.dot_general(
            wide, queries, (((1,), (1,)), ((), ())), preferred_element_type=f32
        )
        weight = (
            plus.astype(f32) * jnp.tanh(0.5 * logits) + minus.astype(f32)
        ).astype(bf16)
        for ahead in (1, 2) if stop == stops - 3 else (1,) if 0 < stop < stops - 2 else ():
            prepare(stop + ahead, weight)
        state = state - learn_rate * jnp.dot(weight, queries, preferred_element_type=f32)
        if stop + 1 < stops:
            moving = 1 - mine
            route = [(i, (i + 2) % n) for i in range(n) if i % 2 == moving]
            came = lax.ppermute(state.astype(bf16), "cand", route)
        parts[mine].append((weight, wide))
        if stop == 2:
            nothing = weight[0, 0] * 0
            x_own, x_sib = x_own + nothing, x_sib + nothing
        if stop >= stops - 4:
            together = list(zip(*parts[mine]))
            part = lax.dot_general(
                jnp.concatenate(together[0], 0),
                jnp.concatenate(together[1], 0),
                (((0,), (0,)), ((), ())),
                preferred_element_type=f32,
            )
            acc[mine] = part if acc[mine] is None else (acc[mine] + part).astype(bf16)
            parts[mine] = []
            if stop == stops - 4:
                came, acc[mine] = lax.optimization_barrier((came, acc[mine]))
            if stop == stops - 2:
                came, *acc = lax.optimization_barrier((came, *acc))
        if stop == 0:
            came, q_sib = lax.optimization_barrier((came, q_sib))
        if stop + 1 < stops:
            state = jnp.where(odd == (moving == 1), came.astype(f32), state)

    g_own, g_sib = acc
    raw = [
        relation_terms((x_own, x_sib), (g_own, g_sib), (starts, starts_sib), (counts, counts_sib), rel_dev, which)
        for which in range(rel_dev)
    ]
    came = [swap(send, 1) for _, send in raw]
    for i in range(rel_dev - 1):
        came[i], *raw[i + 1] = lax.optimization_barrier((came[i], *raw[i + 1]))
    waves = [[add_halves(keep[c], other[c]) for c in range(2)] for (keep, _), other in zip(raw, came)]
    begun = [part[1] for wave in waves for part in wave]
    query_grad = add(g_own, swap(g_sib, 1))
    query_grad, state, _ = lax.optimization_barrier((query_grad, state, begun))
    back = project(query_grad, starts, counts, relations, near, far, True, False)
    for step in range(steps):
        came = [[swap(part[1], order[step]) for part, order in zip(wave, bit_orders())] for wave in waves]
        if step == 0:
            came, back = lax.optimization_barrier((came, back))
        if step + 1 < steps:
            waves = [[add_halves(part[0], c) for part, c in zip(*both)] for both in zip(waves, came)]
    pairs = []
    for wave, other in zip(waves, came):
        parts = [add_halves(part[0][0], c[0]) for part, c in zip(wave, other)]
        pairs.append([jnp.concatenate(both, -1) for both in zip(*parts)])
    source_grad = []
    for i, bit in enumerate(rel_bits()):
        came = [swap_rel(send, bit) for _, send in pairs]
        if i < 2:
            sorted_rows, _ = lax.optimization_barrier((back, [send for _, send in pairs]))
            source_grad.append(
                lax.dot_general(
                    places_of(place[i * src_rows // 2 : (i + 1) * src_rows // 2], rows),
                    sorted_rows,
                    (((0,), (0,)), ((), ())),
                    preferred_element_type=f32,
                ).astype(bf16)
            )
            came, source_grad[i] = lax.optimization_barrier((came, source_grad[i]))
        if pairs[0][0].shape[0] > 1:
            pairs = [add_halves(keep, other) for (keep, _), other in zip(pairs, came)]
    relation_grad = jnp.stack(
        [keep[0].astype(f32) + other[0].astype(f32) for (keep, _), other in zip(pairs, came)], 1
    )
    source_grad = jnp.concatenate(source_grad, 0)
    updated = swap(state, 1) if stops % 2 == 0 else state
    return updated, source_grad, relation_grad


def solution(mesh):
    placed = (
        P(("cand", "rel"), None),
        P(("cand", "rel"), None),
        P("rel", None, None),
        P(("cand", "rel"), None),
        P(("cand", "rel")),
        P(None, ("cand", "rel"), None),
    )
    return jax.shard_map(
        shards,
        mesh=mesh,
        in_specs=placed,
        out_specs=(P(("cand", "rel"), None), P(("cand", "rel"), None), P("cand", "rel", None)),
        check_vma=False,
    )
```
